256 devices in a mesh: ctx: 4 (over y), cache: 32 (over z, x_lo, core), head: 2 (over x_hi).
Axes of the slice: x: 4 (x_hi: 2, x_lo: 2; x = x_hi * 2 + x_lo), y: 4, z: 8, core: 2. Of those that a mesh axis runs over, the one named last changes fastest.
Arguments:
- queries: bfloat16 [32, 768, 4096], P('cache', 'ctx', 'head'), may hold values from -8 to 8
- fresh_kv: bfloat16 [32, 768, 4, 256], P('cache', 'ctx', 'head'), may hold values from -5 to 5
- kv_store: bfloat16 [2048, 32, 4, 256], P('cache', None, 'head'), may hold values from -6 to 6
- page_owner: int32 [32, 128, 1], P('cache'), may hold values from 0 to 31; in each aligned block of 32 rows (0 to 31, 32 to 63, ..., all dimensions but the last counted through in order) at most 2 rows name the same one
- page_slot: int32 [32, 128], P('cache'), may hold values from 0 to 63
- rec_index: int32 [32, 768], P('cache'), may hold values from 0 to 1023, as said below
Outputs:
- attended: bfloat16 [32, 768, 4096], P('cache', 'ctx', 'head')
The draws below stay inside these ranges and needn't reach their ends.
Inputs may be any that keep to these rules, and one draw needn't show every extreme that they name: `page_owner`: no shard holds more than 2 of the pages of one block (aligned blocks of 32 rows). `rec_index`: each block of 192 entries holds distinct positions in ascending order; the last is always 1024 - 1.
All inputs are finite; a program needn't handle non-finite values.
Results may differ from the reference program's by a relative error of at most 0.0039.
Values may be sent and summed in bfloat16 or wider, within the bound.
A program may use at most 64 MiB of HBM per device.

```python
import math
import jax
import jax.numpy as jnp
import numpy as np
from jax import lax

QH = 32
KVH = 4
HD = 128
PAGE = 32
TOK_DEV = 1024
STORE_DEV = 64
PAGES_DEV = 32
REC_DEV = 192
CAP = 2
PROMPTS = 32
PAGES_PROMPT = 128
REC_PROMPT = 768
STORE_PAGES = 2048
N_CACHE = 32


def draw_queries(key, part):
    key = jax.random.fold_in(key, 11)
    full_shape = (PROMPTS, REC_PROMPT, QH * HD)
    values = jnp.clip(2.5 * jax.random.normal(key, full_shape, jnp.float32), -8.0, 8.0)
    return values.astype(jnp.bfloat16)


def draw_fresh_kv(key, part):
    key = jax.random.fold_in(key, 23)
    full_shape = (PROMPTS, REC_PROMPT, KVH, 2 * HD)
    values = jnp.clip(jax.random.normal(key, full_shape, jnp.float32), -5.0, 5.0)
    return values.astype(jnp.bfloat16)


def draw_rec_index(key, part):
    key = jax.random.fold_in(key, 37)
    block_count = PROMPTS * (REC_PROMPT // REC_DEV)
    block_keys = jax.random.split(key, block_count)

    def one_block(block_key):
        shuffled = jax.random.permutation(block_key, TOK_DEV - 1).astype(jnp.int32)
        chosen = jnp.sort(shuffled[:REC_DEV - 1])
        return jnp.concatenate([chosen, jnp.full((1,), TOK_DEV - 1, jnp.int32)])
    return jax.vmap(one_block)(block_keys).reshape(PROMPTS, REC_PROMPT).astype(jnp.int32)


def touch_ends(entries, key, low, high):
    spot = [jax.random.randint(jax.random.fold_in(key, axis), (), 0, length) for axis, length in enumerate(entries.shape)]
    main_axis = entries.shape.index(max(entries.shape))
    next_to = spot[:main_axis] + [(spot[main_axis] + 1) % entries.shape[main_axis]] + spot[main_axis + 1:]
    return entries.at[tuple(spot)].set(low).at[tuple(next_to)].set(high)


def block_scale(stream_key, dims, pieces, smallest, largest):
    def one(dim, parts):
        heights = jax.random.uniform(jax.random.fold_in(jax.random.fold_in(stream_key, 6), dim), (parts,), jnp.float32, smallest / len(pieces), largest / len(pieces))
        return jnp.repeat(jnp.exp(heights), dims[dim] // parts).reshape((-1,) + (1,) * (len(dims) - dim - 1))

    factor_of = one(*pieces[0])
    for cut in pieces[1:]:
        factor_of = factor_of * one(*cut)
    return factor_of


def deal_out(key, own, number, rows, number_of, top, bound, lean):
    sequence = jax.random.permutation(key, number_of)
    heavy_load, common = shares(number_of, rows * top, bound, lean, True), shares(number_of, rows * top, bound, lean, False)
    places = jnp.arange(number_of)

    def named(tallies, rotation):
        used = int((tallies > 0).sum())
        fixed = max(1, used // 4)
        passed = fixed + (places - fixed + rotation * (used - fixed)) % max(1, number_of - fixed)
        return jnp.zeros((number_of,), jnp.int32).at[sequence[jnp.where(places < fixed, places, passed)]].set(jnp.asarray(tallies, jnp.int32))

    tallies = jnp.where(number % 4 == 0, named(heavy_load, number // 4), named(common, number - number // 4 - 1))
    mixed = jax.random.permutation(jax.random.fold_in(own, 3), number_of)
    donor, sink = mixed[0:number_of // 2 * 2:2], mixed[1:number_of // 2 * 2:2]
    room = jnp.minimum(tallies[donor] - 1, bound - tallies[sink]) // 2
    room = jnp.where((donor == sequence[0]) | (sink == sequence[0]) | (tallies[sink] == 0), 0, jnp.maximum(room, 0))
    passed = jax.random.randint(jax.random.fold_in(own, 4), (number_of // 2,), 0, 1 << 20) % (room + 1)
    tallies = tallies.at[donor].add(-passed).at[sink].add(passed)
    items = jnp.searchsorted(jnp.cumsum(tallies), jnp.arange(rows * top), side="right").astype(jnp.int32)
    listing = items.reshape(top, rows).T
    listing = listing[jax.random.permutation(jax.random.fold_in(own, 1), rows)]
    rotation = jax.random.randint(jax.random.fold_in(own, 2), (rows, 1), 0, top)
    return jnp.take_along_axis(listing, (jnp.arange(top)[None, :] + rotation) % top, axis=1)


def shares(amount, total, reach, slope, full):
    weights = [(1 << 20) // math.isqrt(grade ** slope) + 1 for grade in range(1, amount + 1)]
    largest = reach if full else min(reach, max(-(-total // amount), total * weights[0] // sum(weights)))
    least = 1 if total - largest >= amount - 1 else 0
    holding, spare = [largest] + [least] * (amount - 1), total - largest - least * (amount - 1)
    while spare > 0:
        candidates = [i for i in range(1, amount) if holding[i] < largest] or [i for i in range(1, amount) if holding[i] < reach]
        whole, remaining = sum([weights[i] for i in candidates]), spare
        for i in candidates:
            addition = min(reach - holding[i], max(1, remaining * weights[i] // whole), spare)
            holding[i] = holding[i] + addition
            spare = spare - addition
    return np.array(holding)


def bell_draw(stream_key, dims, deviation, bound, shards=(), kind=jnp.bfloat16):
    values = deviation * jax.random.normal(stream_key, dims, jnp.float32)
    if shards:
        values = values * block_scale(stream_key, dims, shards, -0.22, 0.18)
    return jnp.clip(values, -bound, bound).astype(kind)


def setup_inputs(seed: int = 0) -> dict:
    keys = jax.random.split(jax.random.key(seed), 7)
    queries = draw_queries(jax.random.fold_in(keys[6], 71), 0)
    fresh_kv = draw_fresh_kv(jax.random.fold_in(keys[6], 71), 0)
    kv_store = bell_draw(keys[2], (STORE_PAGES, PAGE, KVH, 2 * HD), 1.0, 6.0, ((0, 32), (2, 2)))
    page_owner_keys = jax.random.split(jax.random.fold_in(keys[3], 1), PROMPTS * PAGES_PROMPT // PAGES_DEV)
    page_owner_turns = jax.random.permutation(jax.random.fold_in(keys[3], 3), PROMPTS * PAGES_PROMPT // PAGES_DEV)
    page_owner = jax.vmap(lambda own, number: deal_out(jax.random.fold_in(keys[3], 2), own, number, PAGES_DEV, N_CACHE, 1, CAP, 2))(page_owner_keys, page_owner_turns).reshape((PROMPTS, PAGES_PROMPT, 1))
    page_slot = touch_ends(jax.random.randint(keys[4], (PROMPTS, PAGES_PROMPT), 0, STORE_DEV), jax.random.fold_in(keys[4], 1), 0, STORE_DEV - 1).astype(jnp.int32)
    rec_index = draw_rec_index(jax.random.fold_in(keys[6], 71), 0)
    return dict(queries=queries, fresh_kv=fresh_kv, kv_store=kv_store, page_owner=page_owner, page_slot=page_slot, rec_index=rec_index)


def reference(queries, fresh_kv, kv_store, page_owner, page_slot, rec_index):
    group_size = QH // KVH

    def one_prompt(inputs):
        query_rows, fresh_rows, owners, slot_ids, rec_all = inputs
        page_ids = (owners[:, 0] * STORE_DEV + slot_ids).astype(jnp.int32)
        cached = jnp.take(kv_store, page_ids, axis=0).reshape(PAGES_PROMPT * PAGE, KVH, 2 * HD)
        positions = (jnp.arange(REC_PROMPT, dtype=jnp.int32) // REC_DEV) * TOK_DEV + rec_all.astype(jnp.int32)
        merged = cached.at[positions].set(fresh_rows)
        key_pos = jnp.arange(PAGES_PROMPT * PAGE, dtype=jnp.int32)
        visible = key_pos[None, :] <= positions[:, None]
        query_heads = query_rows.reshape(REC_PROMPT, KVH, group_size, HD)

        def one_head(kv_head):
            key_rows = merged[:, kv_head, :HD].astype(jnp.float32)
            value_rows = merged[:, kv_head, HD:].astype(jnp.float32)
            query_part = query_heads[:, kv_head].astype(jnp.float32)
            scores = jnp.einsum("rgh,lh->grl", query_part, key_rows) * (HD ** -0.5)
            masked = jnp.where(visible[None], scores, -jnp.inf)
            row_max = jnp.max(masked, axis=-1, keepdims=True)
            weights = jnp.where(visible[None], jnp.exp(masked - row_max), 0.0)
            row_sum = jnp.sum(weights, axis=-1)
            rounded = lax.optimization_barrier(weights.astype(jnp.bfloat16)).astype(jnp.float32)
            mixed = jnp.einsum("grl,lh->grh", rounded, value_rows)
            return mixed / row_sum[..., None]

        outputs = lax.map(one_head, jnp.arange(KVH, dtype=jnp.int32))
        return outputs.transpose(2, 0, 1, 3).reshape(REC_PROMPT, QH * HD).astype(jnp.bfloat16)

    return lax.map(one_prompt, (queries, fresh_kv, page_owner, page_slot, rec_index))
```

```python
import functools
import math

import jax
import jax.numpy as jnp
from jax import lax
from jax.experimental import pallas as pl
from jax.experimental.pallas import tpu as pltpu
from jax.sharding import PartitionSpec as P

MESH = pl.DeviceIdType.MESH
EMPTY = -1e30
HIDDEN = -2e30
HALVES = 2


def kernel(
    dims, req, idx, rec_row, rec_col, store, fresh, queries, out,
    req_in, req_smem, sendbuf, kv, part, keep, q_all, m_all, l_all, acc_all,
    req_send, req_recv, smem_sem, page_send, page_recv, ctx_send, ctx_recv, *recvbuf,
):
    n, ctx_count, kv_heads, pages, page_len, rows, heads, hd = dims
    pieces = kv_heads * HALVES
    run = page_len // HALVES
    length = pages * run
    group = heads // kv_heads
    me = lax.axis_index("cache")
    c = lax.axis_index("ctx")

    barrier = pltpu.get_barrier_semaphore()

    def greet(k, _):
        pl.semaphore_signal(barrier, inc=1, device_id={"cache": lax.rem(me + k, n)}, device_id_type=MESH)
        return 0

    lax.fori_loop(1, n, greet, 0)
    for step in (1, ctx_count - 1):
        pl.semaphore_signal(barrier, inc=1, device_id={"ctx": lax.rem(c + step, ctx_count)}, device_id_type=MESH)
    pl.semaphore_wait(barrier, n + 1)

    def ask(k, _):
        d = lax.rem(me + k, n)
        pltpu.make_async_remote_copy(
            req.at[d], req_in.at[me], req_send, req_recv, device_id={"cache": d}, device_id_type=MESH
        ).start()
        return 0

    lax.fori_loop(1, n, ask, 0)
    req_in[me] = req[me]

    fresh_pos = rec_row[...]
    for half in range(HALVES):
        local = lax.broadcasted_iota(jnp.int32, (length, rows), 0)
        pos = (local // run) * page_len + half * run + local % run
        hit = jnp.where(pos == fresh_pos, 1.0, 0.0)
        covered = jnp.sum(hit, axis=1, keepdims=True)
        keep[half] = jnp.broadcast_to(1.0 - covered, (length, 2 * hd)).astype(jnp.bfloat16)
        one_hot = hit.astype(jnp.bfloat16)
        for k in range(kv_heads):
            part[k * HALVES + half] = jnp.dot(
                one_hot, fresh[k], preferred_element_type=jnp.float32
            ).astype(jnp.bfloat16)
    for g in range(heads):
        q_all[g] = queries[:, g * hd : (g + 1) * hd]
    m_all[...] = jnp.full(m_all.shape, EMPTY, jnp.float32)
    l_all[...] = jnp.zeros(l_all.shape, jnp.float32)
    acc_all[...] = jnp.zeros(acc_all.shape, jnp.float32)

    others = req_in.at[pl.ds(0, n - 1)]
    pltpu.make_async_copy(others, others, req_recv).wait()
    to_smem = pltpu.make_async_copy(req_in, req_smem, smem_sem)
    to_smem.start()
    to_smem.wait()

    for q in range(pieces):

        def fill(d, q=q):
            for r in range(2):
                sendbuf[q, d, r] = store[req_smem[d, 0, r] * pieces + q]

        def give(k, _, q=q, fill=fill):
            d = lax.rem(me + k, n)
            fill(d)
            pltpu.make_async_remote_copy(
                sendbuf.at[q, d], recvbuf[q].at[me], page_send.at[q], page_recv.at[q],
                device_id={"cache": d}, device_id_type=MESH,
            ).start()
            return 0

        lax.fori_loop(1, n, give, 0)
        for r in range(2):
            recvbuf[q][me, r] = store[req_smem[me, 0, r] * pieces + q]

    factor = hd**-0.5 * math.log2(math.e)

    def attend(q, block, own):
        def one(g, _):
            keys, values = kv[q * ctx_count + block, :, :hd], kv[q * ctx_count + block, :, hd:]
            scores = lax.dot_general(
                q_all[g], keys, (((1,), (1,)), ((), ())), preferred_element_type=jnp.float32
            )
            if own:
                local = lax.broadcasted_iota(jnp.int32, (rows, length), 1)
                pos = (local // run) * page_len + (q % HALVES) * run + local % run
                scores = jnp.where(pos <= rec_col[...], scores, HIDDEN)
            m_old = m_all[g]
            m_new = jnp.maximum(m_old, jnp.max(scores, axis=1, keepdims=True))
            alpha = jnp.exp2((m_old - m_new) * factor)
            weights = jnp.exp2((scores - m_new[:, :1]) * factor)
            l_all[g] = l_all[g] * alpha + jnp.sum(weights, axis=1, keepdims=True)
            acc_all[g] = acc_all[g] * alpha + jnp.dot(
                weights.astype(jnp.bfloat16), values, preferred_element_type=jnp.float32
            )
            m_all[g] = m_new
            return 0

        k = q // HALVES
        lax.fori_loop(k * group, (k + 1) * group, one, 0)

    def along(q, block, sem, to):
        ref = kv.at[q * ctx_count + block]
        return pltpu.make_async_remote_copy(
            ref, ref, ctx_send.at[q, sem], ctx_recv.at[q, block], device_id={"ctx": to}, device_id_type=MESH
        )

    for q in range(pieces):
        others = recvbuf[q].at[pl.ds(0, n - 1)]
        pltpu.make_async_copy(others, others, page_recv.at[q]).wait()

        def place(j, _, q=q):
            at = idx[j]
            spot = pl.ds(pl.multiple_of(j * run, run), run)
            page = recvbuf[q][at // 2, at % 2]
            kv[q * ctx_count + c, spot, :] = page * keep[q % HALVES, spot, :] + part[q, spot, :]
            return 0

        lax.fori_loop(0, pages, place, 0)

        @pl.when(c < ctx_count - 1)
        def _():
            along(q, c, 0, c + 1).start()

        @pl.when(c == 0)
        def _():
            along(q, c, 1, ctx_count - 1).start()

        attend(q, c, True)
        for t in range(ctx_count - 1):

            @pl.when(t < c)
            def _(t=t, q=q):
                last = c // 3
                block = last * ((3 - t) % 3) + (1 - last) * (c - 1 - t)
                along(q, block, 0, c).wait_recv()
                if t == 0:

                    @pl.when(c >= 2)
                    def _():
                        along(q, block, 2, 5 - c).start()

                attend(q, block, False)

    for g in range(heads):
        out[:, g * hd : (g + 1) * hd] = (acc_all[g] / l_all[g]).astype(out.dtype)

    def sent(q, sem):
        pltpu.make_async_copy(kv.at[0], kv.at[0], ctx_send.at[q, sem]).wait()

    pltpu.make_async_copy(req.at[pl.ds(0, n - 1)], req.at[pl.ds(0, n - 1)], req_send).wait()
    for q in range(pieces):
        most = sendbuf.at[q, pl.ds(0, n - 1)]
        pltpu.make_async_copy(most, most, page_send.at[q]).wait()

        @pl.when(c < ctx_count - 1)
        def _():
            sent(q, 0)

        @pl.when(c == 0)
        def _():
            sent(q, 1)

        @pl.when(c >= 2)
        def _():
            sent(q, 2)


def shards(queries, fresh_kv, kv_store, page_owner, page_slot, rec_index):
    n, ctx_count = lax.axis_size("cache"), lax.axis_size("ctx")
    c = lax.axis_index("ctx")
    rows, kv_heads, hd = queries.shape[1], fresh_kv.shape[2], fresh_kv.shape[3] // 2
    heads = queries.shape[2] // hd
    slots, page_len = kv_store.shape[:2]
    pages = page_owner.shape[1] // ctx_count
    pieces, run = kv_heads * HALVES, page_len // HALVES

    owners = lax.dynamic_slice_in_dim(page_owner[0, :, 0], c * pages, pages)
    slot_ids = lax.dynamic_slice_in_dim(page_slot[0], c * pages, pages)
    rec = lax.dynamic_slice_in_dim(rec_index[0], c * rows, rows)
    order = lax.iota(jnp.int32, pages)
    named = owners[None, :] == lax.iota(jnp.int32, n)[:, None]
    coded = (order * slots + slot_ids)[None, :]
    none = pages * slots
    first = jnp.min(jnp.where(named, coded, none), axis=1) % slots
    last = jnp.max(jnp.where(named, coded, 0), axis=1) % slots
    lane = lax.broadcasted_iota(jnp.int32, (n, 1, 128), 2)
    req = jnp.where(lane == 0, first[:, None, None], last[:, None, None])
    same = owners[None, :] == owners[:, None]
    earliest = jnp.min(jnp.where(same, order[None, :], pages), axis=1)
    idx = owners * 2 + (earliest != order).astype(jnp.int32)

    store = kv_store.transpose(0, 2, 1, 3).reshape(slots * pieces, run, 2 * hd)
    fresh = fresh_kv[0].transpose(1, 0, 2)
    dims = (n, ctx_count, kv_heads, pages, page_len, rows, heads, hd)
    bf16, f32 = jnp.bfloat16, jnp.float32
    vmem, smem = pl.BlockSpec(memory_space=pltpu.VMEM), pl.BlockSpec(memory_space=pltpu.SMEM)
    dma = pltpu.SemaphoreType.DMA
    result = pl.pallas_call(
        functools.partial(kernel, dims),
        out_shape=jax.ShapeDtypeStruct((rows, heads * hd), bf16),
        in_specs=[vmem, smem, vmem, vmem, vmem, vmem, vmem],
        out_specs=vmem,
        scratch_shapes=[
            pltpu.VMEM((n, 1, 128), jnp.int32),
            pltpu.SMEM((n, 1, 128), jnp.int32),
            pltpu.VMEM((pieces, n, 2, run, 2 * hd), bf16),
            pltpu.VMEM((pieces * ctx_count, pages * run, 2 * hd), bf16),
            pltpu.VMEM((pieces, pages * run, 2 * hd), bf16),
            pltpu.VMEM((HALVES, pages * run, 2 * hd), bf16),
            pltpu.VMEM((heads, rows, hd), bf16),
            pltpu.VMEM((heads, rows, 128), f32),
            pltpu.VMEM((heads, rows, 128), f32),
            pltpu.VMEM((heads, rows, hd), f32),
            dma, dma, dma,
            dma((pieces,)), dma((pieces,)),
            dma((pieces, 3)), dma((pieces, ctx_count)),
            *[pltpu.VMEM((n, 2, run, 2 * hd), bf16) for _ in range(pieces)],
        ],
        compiler_params=pltpu.CompilerParams(
            collective_id=0, has_side_effects=True, vmem_limit_bytes=48 * 1024 * 1024
        ),
    )(req, idx, rec[None, :], rec[:, None], store, fresh, queries[0])
    return result[None]


def solution(mesh):
    in_specs = (
        P("cache", "ctx", "head"),
        P("cache", "ctx", "head", None),
        P("cache", None, "head", None),
        P("cache", None, None),
        P("cache", None),
        P("cache", None),
    )
    out_specs = P("cache", "ctx", "head")
    return jax.shard_map(shards, mesh=mesh, in_specs=in_specs, out_specs=out_specs, check_vma=False)
```

```python
import functools
import math

import jax
import jax.numpy as jnp
from jax import lax
from jax.experimental import pallas as pl
from jax.experimental.pallas import tpu as pltpu
from jax.sharding import PartitionSpec as P

MESH = pl.DeviceIdType.MESH
EMPTY = -1e30
HIDDEN = -2e30
HALVES = 2


def kernel(
    dims, req, idx, rec_row, rec_tiled, store, fresh, queries, out,
    req_in, req_smem, sendbuf, kv, v_rows, part, keep, stack, q_t, m_all, l_all, acc_all,
    req_send, req_recv, smem_sem, page_send, page_recv, ctx_send, ctx_recv, *recvbuf,
):
    n, ctx_count, kv_heads, pages, page_len, rows, heads, hd = dims
    pieces = kv_heads * HALVES
    run = page_len // HALVES
    length = pages * run
    group = heads // kv_heads
    me = lax.axis_index("cache")
    c = lax.axis_index("ctx")

    barrier = pltpu.get_barrier_semaphore()

    def greet(k, _):
        pl.semaphore_signal(barrier, inc=1, device_id={"cache": lax.rem(me + k, n)}, device_id_type=MESH)
        return 0

    lax.fori_loop(1, n, greet, 0)
    for step in (1, ctx_count - 1):
        pl.semaphore_signal(barrier, inc=1, device_id={"ctx": lax.rem(c + step, ctx_count)}, device_id_type=MESH)
    pl.semaphore_wait(barrier, n + 1)

    def ask(k, _):
        d = lax.rem(me + k, n)
        pltpu.make_async_remote_copy(
            req.at[d], req_in.at[me], req_send, req_recv, device_id={"cache": d}, device_id_type=MESH
        ).start()
        return 0

    lax.fori_loop(1, n, ask, 0)
    req_in[me] = req[me]

    others = req_in.at[pl.ds(0, n - 1)]
    pltpu.make_async_copy(others, others, req_recv).wait()
    to_smem = pltpu.make_async_copy(req_in, req_smem, smem_sem)
    to_smem.start()
    to_smem.wait()

    for q in range(pieces):

        def fill(d, q=q):
            for r in range(2):
                sendbuf[q, d, r] = store[req_smem[d, 0, r] * pieces + q]

        def give(k, _, q=q, fill=fill):
            d = lax.rem(me + k, n)
            fill(d)
            pltpu.make_async_remote_copy(
                sendbuf.at[q, d], recvbuf[q].at[me], page_send.at[q], page_recv.at[q],
                device_id={"cache": d}, device_id_type=MESH,
            ).start()
            return 0

        lax.fori_loop(1, n, give, 0)
        for r in range(2):
            recvbuf[q][me, r] = store[req_smem[me, 0, r] * pieces + q]

    fresh_pos = rec_row[...]
    for half in range(HALVES):
        local = lax.broadcasted_iota(jnp.int32, (length, rows), 0)
        pos = (local // run) * page_len + half * run + local % run
        hit = jnp.where(pos == fresh_pos, 1.0, 0.0)
        covered = jnp.sum(hit, axis=1, keepdims=True)
        keep[half] = jnp.broadcast_to(1.0 - covered, (length, 2 * hd)).astype(jnp.bfloat16)
        one_hot = hit.astype(jnp.bfloat16)
        for k in range(kv_heads):
            part[k * HALVES + half] = jnp.dot(
                one_hot, fresh[k], preferred_element_type=jnp.float32
            ).astype(jnp.bfloat16)

    columns = group * rows
    for g in range(heads):
        at = (g % group) * rows
        stack[g // group, at : at + rows, :] = queries[:, g * hd : (g + 1) * hd]
    for k in range(kv_heads):
        for at in range(0, columns, 128):
            block = stack[k, at : at + 128, :].astype(jnp.float32)
            q_t[k, :, at : at + 128] = block.T.astype(jnp.bfloat16)
    m_all[...] = jnp.full(m_all.shape, EMPTY, jnp.float32)
    l_all[...] = jnp.zeros(l_all.shape, jnp.float32)
    acc_all[...] = jnp.zeros(acc_all.shape, jnp.float32)

    factor = hd**-0.5 * math.log2(math.e)

    def attend(q, block, own):
        k = q // HALVES
        at = q * ctx_count + block
        keys = kv[at, :length, :]
        values = jnp.concatenate(
            [kv[at, length + i : length + i + 128, :] for i in range(0, length, 128)], axis=1
        )
        scores = jnp.dot(keys, q_t[k], preferred_element_type=jnp.float32)
        if own:
            local = lax.broadcasted_iota(jnp.int32, (length, 1), 0)
            pos = (local // run) * page_len + (q % HALVES) * run + local % run
            scores = jnp.where(pos <= rec_tiled[...], scores, HIDDEN)
        m_old = m_all[k]
        m_new = jnp.maximum(m_old, jnp.max(scores, axis=0, keepdims=True))
        alpha = jnp.exp2((m_old - m_new) * factor)
        weights = jnp.exp2((scores - m_new[:1]) * factor)
        l_all[k] = l_all[k] * alpha + jnp.sum(weights, axis=0, keepdims=True)
        acc_all[k] = acc_all[k] * alpha[:1] + jnp.dot(
            values, weights.astype(jnp.bfloat16), preferred_element_type=jnp.float32
        )
        m_all[k] = m_new

    halves = (pl.ds(0, length), pl.ds(length, length))
    whole = pl.ds(0, 2 * length)

    def along(q, block, span, sem, flag, to):
        ref = kv.at[q * ctx_count + block, span]
        return pltpu.make_async_remote_copy(
            ref, ref, ctx_send.at[q, sem], ctx_recv.at[q, block, flag],
            device_id={"ctx": to}, device_id_type=MESH,
        )

    for q in range(pieces):
        others = recvbuf[q].at[pl.ds(0, n - 1)]
        pltpu.make_async_copy(others, others, page_recv.at[q]).wait()

        def place(j, _, q=q):
            at = idx[j]
            spot = pl.ds(pl.multiple_of(j * run, run), run)
            page = recvbuf[q][at // 2, at % 2] * keep[q % HALVES, spot, :] + part[q, spot, :]
            kv[q * ctx_count + c, spot, :] = page[:, :hd]
            v_rows[spot, :] = page[:, hd:]
            return 0

        lax.fori_loop(0, pages, place, 0)
        for i in range(0, length, 128):
            block = v_rows[i : i + 128, :].astype(jnp.float32)
            kv[q * ctx_count + c, length + i : length + i + 128, :] = block.T.astype(jnp.bfloat16)

        @pl.when(c == 0)
        def _(q=q):
            along(q, 0, whole, 1, 0, 3).start()
            along(q, 0, whole, 0, 0, 1).start()

        @pl.when(c == 1)
        def _(q=q):
            along(q, 1, halves[1], 2, 1, 0).start()
            along(q, 1, halves[0], 0, 0, 2).start()
            along(q, 1, halves[1], 1, 1, 2).start()

        @pl.when(c == 2)
        def _(q=q):
            along(q, 2, whole, 0, 0, 3).start()

        attend(q, c, True)

        @pl.when(c == 0)
        def _(q=q):
            along(q, 1, halves[1], 2, 1, 0).wait_recv()
            along(q, 1, halves[1], 2, 1, 3).start()

        def earlier(t, _, q=q):
            last = c // 3
            block = last * ((3 - t) % 3) + (1 - last) * (c - 1 - t)

            @pl.when(block == 1)
            def _():
                along(q, 1, halves[0], 0, 0, c).wait_recv()

                @pl.when(c == 2)
                def _():
                    along(q, 1, halves[0], 1, 0, 3).start()

                along(q, 1, halves[1], 1, 1, c).wait_recv()

            @pl.when(block != 1)
            def _():
                along(q, block, whole, 0, 0, c).wait_recv()

                @pl.when((c == 3) & (block == 0))
                def _():
                    along(q, 0, whole, 0, 0, 2).start()

            attend(q, block, False)
            return 0

        lax.fori_loop(0, c, earlier, 0)

    for k in range(kv_heads):
        for at in range(0, columns, 128):
            span = slice(at, at + 128)
            stack[k, span, :] = (acc_all[k, :, span] / l_all[k, :1, span]).T.astype(jnp.bfloat16)
    for g in range(heads):
        at = (g % group) * rows
        out[:, g * hd : (g + 1) * hd] = stack[g // group, at : at + rows, :]

    pltpu.make_async_copy(req.at[pl.ds(0, n - 1)], req.at[pl.ds(0, n - 1)], req_send).wait()
    for q in range(pieces):
        most = sendbuf.at[q, pl.ds(0, n - 1)]
        pltpu.make_async_copy(most, most, page_send.at[q]).wait()

        @pl.when(c == 0)
        def _(q=q):
            along(q, 0, whole, 0, 0, 1).wait_send()
            along(q, 0, whole, 1, 0, 3).wait_send()
            along(q, 1, halves[1], 2, 1, 3).wait_send()

        @pl.when(c == 1)
        def _(q=q):
            along(q, 1, halves[0], 0, 0, 2).wait_send()
            along(q, 1, halves[1], 1, 1, 2).wait_send()
            along(q, 1, halves[1], 2, 1, 0).wait_send()

        @pl.when(c == 2)
        def _(q=q):
            along(q, 2, whole, 0, 0, 3).wait_send()
            along(q, 1, halves[0], 1, 0, 3).wait_send()

        @pl.when(c == 3)
        def _(q=q):
            along(q, 0, whole, 0, 0, 2).wait_send()


def shards(queries, fresh_kv, kv_store, page_owner, page_slot, rec_index):
    n, ctx_count = lax.axis_size("cache"), lax.axis_size("ctx")
    c = lax.axis_index("ctx")
    rows, kv_heads, hd = queries.shape[1], fresh_kv.shape[2], fresh_kv.shape[3] // 2
    heads = queries.shape[2] // hd
    slots, page_len = kv_store.shape[:2]
    pages = page_owner.shape[1] // ctx_count
    pieces, run = kv_heads * HALVES, page_len // HALVES

    owners = lax.dynamic_slice_in_dim(page_owner[0, :, 0], c * pages, pages)
    slot_ids = lax.dynamic_slice_in_dim(page_slot[0], c * pages, pages)
    rec = lax.dynamic_slice_in_dim(rec_index[0], c * rows, rows)
    order = lax.iota(jnp.int32, pages)
    named = owners[None, :] == lax.iota(jnp.int32, n)[:, None]
    coded = (order * slots + slot_ids)[None, :]
    none = pages * slots
    first = jnp.min(jnp.where(named, coded, none), axis=1) % slots
    last = jnp.max(jnp.where(named, coded, 0), axis=1) % slots
    lane = lax.broadcasted_iota(jnp.int32, (n, 1, 128), 2)
    req = jnp.where(lane == 0, first[:, None, None], last[:, None, None])
    same = owners[None, :] == owners[:, None]
    earliest = jnp.min(jnp.where(same, order[None, :], pages), axis=1)
    idx = owners * 2 + (earliest != order).astype(jnp.int32)

    store = kv_store.transpose(0, 2, 1, 3).reshape(slots * pieces, run, 2 * hd)
    fresh = fresh_kv[0].transpose(1, 0, 2)
    columns = heads // kv_heads * rows
    dims = (n, ctx_count, kv_heads, pages, page_len, rows, heads, hd)
    bf16, f32 = jnp.bfloat16, jnp.float32
    vmem, smem = pl.BlockSpec(memory_space=pltpu.VMEM), pl.BlockSpec(memory_space=pltpu.SMEM)
    dma = pltpu.SemaphoreType.DMA
    result = pl.pallas_call(
        functools.partial(kernel, dims),
        out_shape=jax.ShapeDtypeStruct((rows, heads * hd), bf16),
        in_specs=[vmem, smem, vmem, vmem, vmem, vmem, vmem],
        out_specs=vmem,
        scratch_shapes=[
            pltpu.VMEM((n, 1, 128), jnp.int32),
            pltpu.SMEM((n, 1, 128), jnp.int32),
            pltpu.VMEM((pieces, n, 2, run, 2 * hd), bf16),
            pltpu.VMEM((pieces * ctx_count, 2 * pages * run, hd), bf16),
            pltpu.VMEM((pages * run, hd), bf16),
            pltpu.VMEM((pieces, pages * run, 2 * hd), bf16),
            pltpu.VMEM((HALVES, pages * run, 2 * hd), bf16),
            pltpu.VMEM((kv_heads, columns, hd), bf16),
            pltpu.VMEM((kv_heads, hd, columns), bf16),
            pltpu.VMEM((kv_heads, 8, columns), f32),
            pltpu.VMEM((kv_heads, 8, columns), f32),
            pltpu.VMEM((kv_heads, hd, columns), f32),
            dma, dma, dma,
            dma((pieces,)), dma((pieces,)),
            dma((pieces, 3)), dma((pieces, ctx_count, 2)),
            *[pltpu.VMEM((n, 2, run, 2 * hd), bf16) for _ in range(pieces)],
        ],
        compiler_params=pltpu.CompilerParams(
            collective_id=0, has_side_effects=True, vmem_limit_bytes=48 * 1024 * 1024
        ),
    )(req, idx, rec[None, :], jnp.tile(rec, heads // kv_heads)[None, :], store, fresh, queries[0])
    return result[None]


def solution(mesh):
    in_specs = (
        P("cache", "ctx", "head"),
        P("cache", "ctx", "head", None),
        P("cache", None, "head", None),
        P("cache", None, None),
        P("cache", None),
        P("cache", None),
    )
    out_specs = P("cache", "ctx", "head")
    return jax.shard_map(shards, mesh=mesh, in_specs=in_specs, out_specs=out_specs, check_vma=False)
```

```python
import functools
import math

import jax
import jax.numpy as jnp
from jax import lax
from jax.experimental import pallas as pl
from jax.experimental.pallas import tpu as pltpu
from jax.sharding import PartitionSpec as P

MESH = pl.DeviceIdType.MESH
EMPTY = -1e30
HIDDEN = -2e30
HALVES = 2


def kernel(
    dims, owner_col, slot_row, rec_in, raw_in, fresh_in, queries_in, out,
    req, req_in, req_smem, idx_rows, idx, raw, fresh_raw, queries, store, sendbuf, kv, v_rows, rec_tiled,
    fresh, part, keep, stack, q_t, m_all, l_all, acc_all,
    load_sem, req_send, req_recv, smem_sem, page_send, page_recv, ctx_send, ctx_recv, *recvbuf,
):
    n, ctx_count, kv_heads, slots, pages, page_len, rows, heads, hd = dims
    parts = kv_heads * HALVES
    pieces = parts * 2
    run = page_len // HALVES
    length = pages * run
    group = heads // kv_heads
    columns = group * rows
    pages_all = pages * ctx_count
    i32 = jnp.int32
    me = lax.axis_index("cache")
    c = lax.axis_index("ctx")

    barrier = pltpu.get_barrier_semaphore()

    def greet(k, _):
        pl.semaphore_signal(barrier, inc=1, device_id={"cache": lax.rem(me + k, n)}, device_id_type=MESH)
        return 0

    lax.fori_loop(1, n, greet, 0)
    for step in (1, ctx_count - 1):
        pl.semaphore_signal(barrier, inc=1, device_id={"ctx": lax.rem(c + step, ctx_count)}, device_id_type=MESH)

    loads = [
        pltpu.make_async_copy(src, dst, load_sem.at[i])
        for i, (src, dst) in enumerate(((raw_in, raw), (fresh_in, fresh_raw), (queries_in, queries)))
    ]
    for load in loads:
        load.start()

    a = lax.broadcasted_iota(i32, (pages_all, pages_all), 0)
    b = lax.broadcasted_iota(i32, (pages_all, pages_all), 1)
    owner_of_a = jnp.broadcast_to(owner_col[...], (pages_all, pages_all))
    owner_row = jnp.sum(jnp.where(a == b, owner_of_a, 0), axis=0, keepdims=True)
    low = c * pages
    before = (owner_of_a == owner_row) & (a < b) & (a >= low)
    second = jnp.max(jnp.where(before, 1, 0), axis=0, keepdims=True)
    idx_rows[...] = jnp.broadcast_to(owner_row * 2 + second, idx_rows.shape)
    to_idx = pltpu.make_async_copy(idx_rows, idx, smem_sem.at[0])
    to_idx.start()

    shard = lax.broadcasted_iota(i32, (n, pages_all), 0)
    place_of = lax.broadcasted_iota(i32, (n, pages_all), 1)
    named = (shard == owner_row) & (place_of >= low) & (place_of < low + pages)
    coded = (place_of * slots + slot_row[...]).astype(jnp.float32)
    first = jnp.min(jnp.where(named, coded, float(pages_all * slots)), axis=1, keepdims=True)
    final = jnp.max(jnp.where(named, coded, 0.0), axis=1, keepdims=True)
    asked = jnp.where(place_of == 0, first, final).astype(i32) % slots
    for d in range(n):
        req[d] = asked[d : d + 1, :]

    loads[0].wait()

    def split(p, _):
        store[pl.ds(p * kv_heads, kv_heads)] = jnp.swapaxes(raw[p], 0, 1)
        return 0

    lax.fori_loop(0, slots, split, 0)
    to_idx.wait()
    pl.semaphore_wait(barrier, n + 1)

    def ask(k, _):
        d = lax.rem(me + k, n)
        pltpu.make_async_remote_copy(
            req.at[d], req_in.at[me], req_send, req_recv, device_id={"cache": d}, device_id_type=MESH
        ).start()
        return 0

    lax.fori_loop(1, n, ask, 0)
    req_in[me] = req[me]

    others = req_in.at[pl.ds(0, n - 1)]
    pltpu.make_async_copy(others, others, req_recv).wait()
    to_smem = pltpu.make_async_copy(req_in, req_smem, smem_sem.at[1])
    to_smem.start()
    to_smem.wait()

    def piece_of(q):
        half, which = q // 2 % HALVES, q % 2
        return q // (2 * HALVES), slice(half * run, (half + 1) * run), slice(which * hd, (which + 1) * hd)

    for q in range(pieces):
        k, span, lanes = piece_of(q)

        def page(d, r, k=k, span=span, lanes=lanes):
            return store[req_smem[d, 0, r] * kv_heads + k, span, lanes]

        def give(step, _, q=q, page=page):
            d = lax.rem(me + step, n)
            for r in range(2):
                sendbuf[q, d, r] = page(d, r)
            pltpu.make_async_remote_copy(
                sendbuf.at[q, d], recvbuf[q].at[me], page_send.at[q], page_recv.at[q],
                device_id={"cache": d}, device_id_type=MESH,
            ).start()
            return 0

        lax.fori_loop(1, n, give, 0)
        for r in range(2):
            recvbuf[q][me, r] = page(me, r)

    fresh_pos = jnp.zeros((1, rows), i32)
    for other in range(ctx_count):
        theirs = rec_in[:, other * rows : (other + 1) * rows]
        fresh_pos = jnp.where(c == other, theirs, fresh_pos)
    for g in range(group):
        rec_tiled[:, g * rows : (g + 1) * rows] = fresh_pos
    loads[1].wait()
    by_head = jnp.swapaxes(fresh_raw[...], 0, 1)
    for k in range(kv_heads):
        fresh[k] = by_head[k]
    loads[2].wait()
    for half in range(HALVES):
        local = lax.broadcasted_iota(jnp.int32, (length, rows), 0)
        pos = (local // run) * page_len + half * run + local % run
        hit = jnp.where(pos == fresh_pos, 1.0, 0.0)
        covered = jnp.sum(hit, axis=1, keepdims=True)
        keep[half] = jnp.broadcast_to(1.0 - covered, (length, hd)).astype(jnp.bfloat16)
        one_hot = hit.astype(jnp.bfloat16)
        for k in range(kv_heads):
            part[k * HALVES + half] = jnp.dot(
                one_hot, fresh[k], preferred_element_type=jnp.float32
            ).astype(jnp.bfloat16)

    for g in range(heads):
        at = (g % group) * rows
        stack[g // group, at : at + rows, :] = queries[:, g * hd : (g + 1) * hd]
    for k in range(kv_heads):
        for at in range(0, columns, 128):
            block = stack[k, at : at + 128, :].astype(jnp.float32)
            q_t[k, :, at : at + 128] = block.T.astype(jnp.bfloat16)
    m_all[...] = jnp.full(m_all.shape, EMPTY, jnp.float32)
    l_all[...] = jnp.zeros(l_all.shape, jnp.float32)
    acc_all[...] = jnp.zeros(acc_all.shape, jnp.float32)

    factor = hd**-0.5 * math.log2(math.e)

    def attend(q, block, own):
        k = q // HALVES
        at = q * ctx_count + block
        keys = kv[at, :length, :]
        values = jnp.concatenate(
            [kv[at, length + i : length + i + 128, :] for i in range(0, length, 128)], axis=1
        )
        scores = jnp.dot(keys, q_t[k], preferred_element_type=jnp.float32)
        if own:
            local = lax.broadcasted_iota(jnp.int32, (length, 1), 0)
            pos = (local // run) * page_len + (q % HALVES) * run + local % run
            scores = jnp.where(pos <= rec_tiled[...], scores, HIDDEN)
        m_old = m_all[k]
        m_new = jnp.maximum(m_old, jnp.max(scores, axis=0, keepdims=True))
        alpha = jnp.exp2((m_old - m_new) * factor)
        weights = jnp.exp2((scores - m_new[:1]) * factor)
        l_all[k] = l_all[k] * alpha + jnp.sum(weights, axis=0, keepdims=True)
        acc_all[k] = acc_all[k] * alpha[:1] + jnp.dot(
            values, weights.astype(jnp.bfloat16), preferred_element_type=jnp.float32
        )
        m_all[k] = m_new

    def along(q, block, sem, to):
        ref = kv.at[q // 2 * ctx_count + block, pl.ds(q % 2 * length, length)]
        return pltpu.make_async_remote_copy(
            ref, ref, ctx_send.at[q, sem], ctx_recv.at[q, block], device_id={"ctx": to}, device_id_type=MESH
        )

    for q in range(pieces):
        others = recvbuf[q].at[pl.ds(0, n - 1)]
        pltpu.make_async_copy(others, others, page_recv.at[q]).wait()
        k, _, lanes = piece_of(q)
        own_part = q // 2 * ctx_count + c

        def place(j, _, q=q, lanes=lanes, own_part=own_part):
            at = idx[0, c * pages + j]
            spot = pl.ds(pl.multiple_of(j * run, run), run)
            page = recvbuf[q][at // 2, at % 2] * keep[q // 2 % HALVES, spot, :] + part[q // 2, spot, lanes]
            if q % 2 == 0:
                kv[own_part, spot, :] = page
            else:
                v_rows[spot, :] = page
            return 0

        lax.fori_loop(0, pages, place, 0)
        if q % 2 == 1:
            for i in range(0, length, 128):
                block = v_rows[i : i + 128, :].astype(jnp.float32)
                kv[own_part, length + i : length + i + 128, :] = block.T.astype(jnp.bfloat16)

        @pl.when(c == 0)
        def _(q=q):
            along(q, 0, 1, 3).start()
            along(q, 0, 0, 1).start()

        @pl.when(c == 1)
        def _(q=q):
            if q % 2 == 1:
                along(q, 1, 1, 0).start()
            along(q, 1, 0, 2).start()

        @pl.when(c == 2)
        def _(q=q):
            along(q, 2, 0, 3).start()

        if q % 2 == 0:
            @pl.when(c == 2)
            def _(q=q):
                along(q, 1, 0, 2).wait_recv()
                along(q, 1, 1, 3).start()

            @pl.when(c == 3)
            def _(q=q):
                along(q, 0, 0, 3).wait_recv()
                along(q, 0, 0, 2).start()

            continue

        attend(q // 2, c, True)

        @pl.when(c == 0)
        def _(q=q):
            along(q, 1, 1, 0).wait_recv()
            along(q, 1, 2, 3).start()

        def earlier(t, _, q=q):
            last = c // 3
            block = last * ((3 - t) % 3) + (1 - last) * (c - 1 - t)

            @pl.when((c == 1) | (t > 0))
            def _():
                along(q - 1, block, 0, c).wait_recv()

            along(q, block, 0, c).wait_recv()

            @pl.when((c == 3) & (t == 0))
            def _():
                along(q, 0, 0, 2).start()

            attend(q // 2, block, False)
            return 0

        lax.fori_loop(0, c, earlier, 0)

    for k in range(kv_heads):
        for at in range(0, columns, 128):
            span = slice(at, at + 128)
            stack[k, span, :] = (acc_all[k, :, span] / l_all[k, :1, span]).T.astype(jnp.bfloat16)
    for g in range(heads):
        at = (g % group) * rows
        out[:, g * hd : (g + 1) * hd] = stack[g // group, at : at + rows, :]

    pltpu.make_async_copy(req.at[pl.ds(0, n - 1)], req.at[pl.ds(0, n - 1)], req_send).wait()
    for q in range(pieces):
        most = sendbuf.at[q, pl.ds(0, n - 1)]
        pltpu.make_async_copy(most, most, page_send.at[q]).wait()

        @pl.when(c == 0)
        def _(q=q):
            along(q, 0, 0, 1).wait_send()
            along(q, 0, 1, 3).wait_send()
            if q % 2 == 1:
                along(q, 1, 2, 3).wait_send()

        @pl.when(c == 1)
        def _(q=q):
            along(q, 1, 0, 2).wait_send()
            if q % 2 == 1:
                along(q, 1, 1, 0).wait_send()

        @pl.when(c == 2)
        def _(q=q):
            along(q, 2, 0, 3).wait_send()
            if q % 2 == 0:
                along(q, 1, 1, 3).wait_send()

        @pl.when(c == 3)
        def _(q=q):
            along(q, 0, 0, 2).wait_send()


def shards(queries, fresh_kv, kv_store, page_owner, page_slot, rec_index):
    n, ctx_count = lax.axis_size("cache"), lax.axis_size("ctx")
    rows, kv_heads, hd = queries.shape[1], fresh_kv.shape[2], fresh_kv.shape[3] // 2
    heads = queries.shape[2] // hd
    slots, page_len = kv_store.shape[:2]
    pages_all = page_owner.shape[1]
    pages = pages_all // ctx_count
    parts, run = kv_heads * HALVES, page_len // HALVES
    pieces, length = 2 * parts, pages * run
    columns = heads // kv_heads * rows
    dims = (n, ctx_count, kv_heads, slots, pages, page_len, rows, heads, hd)
    bf16, f32, i32 = jnp.bfloat16, jnp.float32, jnp.int32
    vmem, anywhere = pl.BlockSpec(memory_space=pltpu.VMEM), pl.BlockSpec(memory_space=pl.ANY)
    dma = pltpu.SemaphoreType.DMA
    result = pl.pallas_call(
        functools.partial(kernel, dims),
        out_shape=jax.ShapeDtypeStruct((rows, heads * hd), bf16),
        in_specs=[vmem, vmem, vmem, anywhere, anywhere, anywhere],
        out_specs=vmem,
        scratch_shapes=[
            pltpu.VMEM((n, 1, 128), i32),
            pltpu.VMEM((n, 1, 128), i32),
            pltpu.SMEM((n, 1, 128), i32),
            pltpu.VMEM((8, pages_all), i32),
            pltpu.SMEM((8, pages_all), i32),
            pltpu.VMEM((slots, page_len, kv_heads, 2 * hd), bf16),
            pltpu.VMEM((rows, kv_heads, 2 * hd), bf16),
            pltpu.VMEM((rows, heads * hd), bf16),
            pltpu.VMEM((slots * kv_heads, page_len, 2 * hd), bf16),
            pltpu.VMEM((pieces, n, 2, run, hd), bf16),
            pltpu.VMEM((parts * ctx_count, 2 * length, hd), bf16),
            pltpu.VMEM((length, hd), bf16),
            pltpu.VMEM((1, columns), i32),
            pltpu.VMEM((kv_heads, rows, 2 * hd), bf16),
            pltpu.VMEM((parts, length, 2 * hd), bf16),
            pltpu.VMEM((HALVES, length, hd), bf16),
            pltpu.VMEM((kv_heads, columns, hd), bf16),
            pltpu.VMEM((kv_heads, hd, columns), bf16),
            pltpu.VMEM((kv_heads, 8, columns), f32),
            pltpu.VMEM((kv_heads, 8, columns), f32),
            pltpu.VMEM((kv_heads, hd, columns), f32),
            dma((3,)), dma, dma, dma((2,)),
            dma((pieces,)), dma((pieces,)),
            dma((pieces, 3)), dma((pieces, ctx_count)),
            *[pltpu.VMEM((n, 2, run, hd), bf16) for _ in range(pieces)],
        ],
        compiler_params=pltpu.CompilerParams(
            collective_id=0, has_side_effects=True, vmem_limit_bytes=48 * 1024 * 1024
        ),
    )(page_owner[0], page_slot, rec_index, kv_store, fresh_kv[0], queries[0])
    return result[None]


def solution(mesh):
    in_specs = (
        P("cache", "ctx", "head"),
        P("cache", "ctx", "head", None),
        P("cache", None, "head", None),
        P("cache", None, None),
        P("cache", None),
        P("cache", None),
    )
    out_specs = P("cache", "ctx", "head")
    return jax.shard_map(shards, mesh=mesh, in_specs=in_specs, out_specs=out_specs, check_vma=False)
```

```python
import functools
import math

import jax
import jax.numpy as jnp
from jax import lax
from jax.experimental import pallas as pl
from jax.experimental.pallas import tpu as pltpu
from jax.sharding import PartitionSpec as P

MESH = pl.DeviceIdType.MESH
EMPTY = -1e30
HIDDEN = -2e30
HALVES = 2


def kernel(
    dims, owner_in, slot_in, rec_hbm, raw_in, fresh_in, queries_in, out,
    owner_row, slot_row, rec_in, req, req_in, req_smem, idx_rows, idx, raw, fresh_raw, queries, store, sendbuf, kv, v_rows, rec_tiled,
    fresh, part, keep, stack, q_t, m_all, l_all, acc_all,
    load_sem, req_send, req_recv, smem_sem, page_send, page_recv, ctx_send, ctx_recv, *recvbuf,
):
    n, ctx_count, kv_heads, slots, pages, page_len, rows, heads, hd = dims
    parts = kv_heads * HALVES
    pieces = parts * 2
    run = page_len // HALVES
    length = pages * run
    group = heads // kv_heads
    columns = group * rows
    pages_all = pages * ctx_count
    i32 = jnp.int32
    me = lax.axis_index("cache")
    c = lax.axis_index("ctx")

    arrays = (
        (owner_in, owner_row), (slot_in, slot_row), (raw_in, raw),
        (rec_hbm, rec_in), (fresh_in, fresh_raw), (queries_in, queries),
    )
    loads = [pltpu.make_async_copy(src, dst, load_sem.at[i]) for i, (src, dst) in enumerate(arrays)]
    for load in loads:
        load.start()

    barrier = pltpu.get_barrier_semaphore()

    def greet(k, _):
        pl.semaphore_signal(barrier, inc=1, device_id={"cache": lax.rem(me + k, n)}, device_id_type=MESH)
        return 0

    lax.fori_loop(1, n, greet, 0)
    for step in (1, ctx_count - 1):
        pl.semaphore_signal(barrier, inc=1, device_id={"ctx": lax.rem(c + step, ctx_count)}, device_id_type=MESH)

    a = lax.broadcasted_iota(i32, (pages_all, pages_all), 0)
    b = lax.broadcasted_iota(i32, (pages_all, pages_all), 1)
    loads[0].wait()
    loads[1].wait()
    owner = owner_row[...]
    owner_f = jnp.broadcast_to(owner, (pages_all, pages_all)).astype(jnp.float32)
    owner_of_a = jnp.sum(jnp.where(a == b, owner_f, 0.0), axis=1, keepdims=True).astype(i32)
    low = c * pages
    before = (owner_of_a == owner) & (a < b) & (a >= low)
    second = jnp.max(jnp.where(before, 1, 0), axis=0, keepdims=True)
    idx_rows[...] = jnp.broadcast_to(owner * 2 + second, idx_rows.shape)
    to_idx = pltpu.make_async_copy(idx_rows, idx, smem_sem.at[0])
    to_idx.start()

    shard = lax.broadcasted_iota(i32, (n, pages_all), 0)
    place_of = lax.broadcasted_iota(i32, (n, pages_all), 1)
    named = (shard == owner) & (place_of >= low) & (place_of < low + pages)
    coded = (place_of * slots + slot_row[...]).astype(jnp.float32)
    first = jnp.min(jnp.where(named, coded, float(pages_all * slots)), axis=1, keepdims=True)
    final = jnp.max(jnp.where(named, coded, 0.0), axis=1, keepdims=True)
    asked = jnp.where(place_of == 0, first, final).astype(i32) % slots
    for d in range(n):
        req[d] = asked[d : d + 1, :]

    loads[2].wait()

    def split(p, _):
        store[pl.ds(p * kv_heads, kv_heads)] = jnp.swapaxes(raw[p], 0, 1)
        return 0

    lax.fori_loop(0, slots, split, 0)
    to_idx.wait()
    pl.semaphore_wait(barrier, n + 1)

    def ask(k, _):
        d = lax.rem(me + k, n)
        pltpu.make_async_remote_copy(
            req.at[d], req_in.at[me], req_send, req_recv, device_id={"cache": d}, device_id_type=MESH
        ).start()
        return 0

    lax.fori_loop(1, n, ask, 0)
    req_in[me] = req[me]

    others = req_in.at[pl.ds(0, n - 1)]
    pltpu.make_async_copy(others, others, req_recv).wait()
    to_smem = pltpu.make_async_copy(req_in, req_smem, smem_sem.at[1])
    to_smem.start()
    to_smem.wait()

    def piece_of(q):
        half, which = q // 2 % HALVES, q % 2
        return q // (2 * HALVES), slice(half * run, (half + 1) * run), slice(which * hd, (which + 1) * hd)

    for q in range(pieces):
        k, span, lanes = piece_of(q)

        def page(d, r, k=k, span=span, lanes=lanes):
            return store[req_smem[d, 0, r] * kv_heads + k, span, lanes]

        def give(step, _, q=q, page=page):
            d = lax.rem(me + step, n)
            for r in range(2):
                sendbuf[q, d, r] = page(d, r)
            pltpu.make_async_remote_copy(
                sendbuf.at[q, d], recvbuf[q].at[me], page_send.at[q], page_recv.at[q],
                device_id={"cache": d}, device_id_type=MESH,
            ).start()
            return 0

        lax.fori_loop(1, n, give, 0)
        for r in range(2):
            recvbuf[q][me, r] = page(me, r)

    loads[3].wait()
    fresh_pos = jnp.zeros((1, rows), i32)
    for other in range(ctx_count):
        theirs = rec_in[:, other * rows : (other + 1) * rows]
        fresh_pos = jnp.where(c == other, theirs, fresh_pos)
    for g in range(group):
        rec_tiled[:, g * rows : (g + 1) * rows] = fresh_pos
    loads[4].wait()
    by_head = jnp.swapaxes(fresh_raw[...], 0, 1)
    for k in range(kv_heads):
        fresh[k] = by_head[k]
    loads[5].wait()
    for half in range(HALVES):
        local = lax.broadcasted_iota(jnp.int32, (length, rows), 0)
        pos = (local // run) * page_len + half * run + local % run
        hit = jnp.where(pos == fresh_pos, 1.0, 0.0)
        covered = jnp.sum(hit, axis=1, keepdims=True)
        keep[half] = jnp.broadcast_to(1.0 - covered, (length, hd)).astype(jnp.bfloat16)
        one_hot = hit.astype(jnp.bfloat16)
        for k in range(kv_heads):
            part[k * HALVES + half] = jnp.dot(
                one_hot, fresh[k], preferred_element_type=jnp.float32
            ).astype(jnp.bfloat16)

    for g in range(heads):
        at = (g % group) * rows
        stack[g // group, at : at + rows, :] = queries[:, g * hd : (g + 1) * hd]
    for k in range(kv_heads):
        for at in range(0, columns, 128):
            block = stack[k, at : at + 128, :].astype(jnp.float32)
            q_t[k, :, at : at + 128] = block.T.astype(jnp.bfloat16)
    m_all[...] = jnp.full(m_all.shape, EMPTY, jnp.float32)
    l_all[...] = jnp.zeros(l_all.shape, jnp.float32)
    acc_all[...] = jnp.zeros(acc_all.shape, jnp.float32)

    factor = hd**-0.5 * math.log2(math.e)

    def attend(q, block, own):
        k = q // HALVES
        at = q * ctx_count + block
        keys = kv[at, :length, :]
        values = jnp.concatenate(
            [kv[at, length + i : length + i + 128, :] for i in range(0, length, 128)], axis=1
        )
        scores = jnp.dot(keys, q_t[k], preferred_element_type=jnp.float32)
        if own:
            local = lax.broadcasted_iota(jnp.int32, (length, 1), 0)
            pos = (local // run) * page_len + (q % HALVES) * run + local % run
            scores = jnp.where(pos <= rec_tiled[...], scores, HIDDEN)
        m_old = m_all[k]
        m_new = jnp.maximum(m_old, jnp.max(scores, axis=0, keepdims=True))
        alpha = jnp.exp2((m_old - m_new) * factor)
        weights = jnp.exp2((scores - m_new[:1]) * factor)
        l_all[k] = l_all[k] * alpha + jnp.sum(weights, axis=0, keepdims=True)
        acc_all[k] = acc_all[k] * alpha[:1] + jnp.dot(
            values, weights.astype(jnp.bfloat16), preferred_element_type=jnp.float32
        )
        m_all[k] = m_new

    def along(q, block, sem, to):
        ref = kv.at[q // 2 * ctx_count + block, pl.ds(q % 2 * length, length)]
        return pltpu.make_async_remote_copy(
            ref, ref, ctx_send.at[q, sem], ctx_recv.at[q, block], device_id={"ctx": to}, device_id_type=MESH
        )

    for q in range(pieces):
        others = recvbuf[q].at[pl.ds(0, n - 1)]
        pltpu.make_async_copy(others, others, page_recv.at[q]).wait()
        k, _, lanes = piece_of(q)
        own_part = q // 2 * ctx_count + c

        def place(j, _, q=q, lanes=lanes, own_part=own_part):
            at = idx[0, c * pages + j]
            spot = pl.ds(pl.multiple_of(j * run, run), run)
            page = recvbuf[q][at // 2, at % 2] * keep[q // 2 % HALVES, spot, :] + part[q // 2, spot, lanes]
            if q % 2 == 0:
                kv[own_part, spot, :] = page
            else:
                v_rows[spot, :] = page
            return 0

        lax.fori_loop(0, pages, place, 0)
        if q % 2 == 1:
            for i in range(0, length, 128):
                block = v_rows[i : i + 128, :].astype(jnp.float32)
                kv[own_part, length + i : length + i + 128, :] = block.T.astype(jnp.bfloat16)

        @pl.when(c == 0)
        def _(q=q):
            along(q, 0, 1, 3).start()
            along(q, 0, 0, 1).start()

        @pl.when(c == 1)
        def _(q=q):
            if q % 2 == 1:
                along(q, 1, 1, 0).start()
            along(q, 1, 0, 2).start()

        @pl.when(c == 2)
        def _(q=q):
            along(q, 2, 0, 3).start()

        if q % 2 == 0:
            @pl.when(c == 2)
            def _(q=q):
                along(q, 1, 0, 2).wait_recv()
                along(q, 1, 1, 3).start()

            @pl.when(c == 3)
            def _(q=q):
                along(q, 0, 0, 3).wait_recv()
                along(q, 0, 0, 2).start()

            continue

        attend(q // 2, c, True)

        @pl.when(c == 0)
        def _(q=q):
            along(q, 1, 1, 0).wait_recv()
            along(q, 1, 2, 3).start()

        def earlier(t, _, q=q):
            last = c // 3
            block = last * ((3 - t) % 3) + (1 - last) * (c - 1 - t)

            @pl.when((c == 1) | (t > 0))
            def _():
                along(q - 1, block, 0, c).wait_recv()

            along(q, block, 0, c).wait_recv()

            @pl.when((c == 3) & (t == 0))
            def _():
                along(q, 0, 0, 2).start()

            attend(q // 2, block, False)
            return 0

        lax.fori_loop(0, c, earlier, 0)

    for k in range(kv_heads):
        for at in range(0, columns, 128):
            span = slice(at, at + 128)
            stack[k, span, :] = (acc_all[k, :, span] / l_all[k, :1, span]).T.astype(jnp.bfloat16)
    for g in range(heads):
        at = (g % group) * rows
        out[:, g * hd : (g + 1) * hd] = stack[g // group, at : at + rows, :]

    pltpu.make_async_copy(req.at[pl.ds(0, n - 1)], req.at[pl.ds(0, n - 1)], req_send).wait()
    for q in range(pieces):
        most = sendbuf.at[q, pl.ds(0, n - 1)]
        pltpu.make_async_copy(most, most, page_send.at[q]).wait()

        @pl.when(c == 0)
        def _(q=q):
            along(q, 0, 0, 1).wait_send()
            along(q, 0, 1, 3).wait_send()
            if q % 2 == 1:
                along(q, 1, 2, 3).wait_send()

        @pl.when(c == 1)
        def _(q=q):
            along(q, 1, 0, 2).wait_send()
            if q % 2 == 1:
                along(q, 1, 1, 0).wait_send()

        @pl.when(c == 2)
        def _(q=q):
            along(q, 2, 0, 3).wait_send()
            if q % 2 == 0:
                along(q, 1, 1, 3).wait_send()

        @pl.when(c == 3)
        def _(q=q):
            along(q, 0, 0, 2).wait_send()


def shards(queries, fresh_kv, kv_store, page_owner, page_slot, rec_index):
    n, ctx_count = lax.axis_size("cache"), lax.axis_size("ctx")
    rows, kv_heads, hd = queries.shape[1], fresh_kv.shape[2], fresh_kv.shape[3] // 2
    heads = queries.shape[2] // hd
    slots, page_len = kv_store.shape[:2]
    pages_all = page_owner.shape[1]
    pages = pages_all // ctx_count
    parts, run = kv_heads * HALVES, page_len // HALVES
    pieces, length = 2 * parts, pages * run
    columns = heads // kv_heads * rows
    dims = (n, ctx_count, kv_heads, slots, pages, page_len, rows, heads, hd)
    bf16, f32, i32 = jnp.bfloat16, jnp.float32, jnp.int32
    vmem, hbm = pl.BlockSpec(memory_space=pltpu.VMEM), pl.BlockSpec(memory_space=pltpu.HBM)
    dma = pltpu.SemaphoreType.DMA
    result = pl.pallas_call(
        functools.partial(kernel, dims),
        out_shape=jax.ShapeDtypeStruct((rows, heads * hd), bf16),
        in_specs=[hbm] * 6,
        out_specs=vmem,
        scratch_shapes=[
            pltpu.VMEM((1, pages_all), i32),
            pltpu.VMEM((1, pages_all), i32),
            pltpu.VMEM(rec_index.shape, i32),
            pltpu.VMEM((n, 1, 128), i32),
            pltpu.VMEM((n, 1, 128), i32),
            pltpu.SMEM((n, 1, 128), i32),
            pltpu.VMEM((8, pages_all), i32),
            pltpu.SMEM((8, pages_all), i32),
            pltpu.VMEM((slots, page_len, kv_heads, 2 * hd), bf16),
            pltpu.VMEM((rows, kv_heads, 2 * hd), bf16),
            pltpu.VMEM((rows, heads * hd), bf16),
            pltpu.VMEM((slots * kv_heads, page_len, 2 * hd), bf16),
            pltpu.VMEM((pieces, n, 2, run, hd), bf16),
            pltpu.VMEM((parts * ctx_count, 2 * length, hd), bf16),
            pltpu.VMEM((length, hd), bf16),
            pltpu.VMEM((1, columns), i32),
            pltpu.VMEM((kv_heads, rows, 2 * hd), bf16),
            pltpu.VMEM((parts, length, 2 * hd), bf16),
            pltpu.VMEM((HALVES, length, hd), bf16),
            pltpu.VMEM((kv_heads, columns, hd), bf16),
            pltpu.VMEM((kv_heads, hd, columns), bf16),
            pltpu.VMEM((kv_heads, 8, columns), f32),
            pltpu.VMEM((kv_heads, 8, columns), f32),
            pltpu.VMEM((kv_heads, hd, columns), f32),
            dma((6,)), dma, dma, dma((2,)),
            dma((pieces,)), dma((pieces,)),
            dma((pieces, 3)), dma((pieces, ctx_count)),
            *[pltpu.VMEM((n, 2, run, hd), bf16) for _ in range(pieces)],
        ],
        compiler_params=pltpu.CompilerParams(
            collective_id=0, has_side_effects=True, vmem_limit_bytes=60 * 1024 * 1024
        ),
    )(page_owner[:, :, 0], page_slot, rec_index, kv_store, fresh_kv[0], queries[0])
    return result[None]


def solution(mesh):
    in_specs = (
        P("cache", "ctx", "head"),
        P("cache", "ctx", "head", None),
        P("cache", None, "head", None),
        P("cache", None, None),
        P("cache", None),
        P("cache", None),
    )
    out_specs = P("cache", "ctx", "head")
    return jax.shard_map(shards, mesh=mesh, in_specs=in_specs, out_specs=out_specs, check_vma=False)
```

```python
import functools
import math

import jax
import jax.numpy as jnp
from jax import lax
from jax.experimental import pallas as pl
from jax.experimental.pallas import tpu as pltpu
from jax.sharding import PartitionSpec as P

MESH = pl.DeviceIdType.MESH
EMPTY = -1e30
HIDDEN = -2e30
HALVES = 2
AHEAD = 3
LEAD = 2
PLANE = 4
SPARE = 2


def kernel(
    dims, shared, owner_in, slot_in, rec_hbm, raw_in, fresh_in, queries_in, out, over,
    owner_row, slot_row, rec_in, req, req_in, req_smem, idx_rows, idx, raw, fresh_raw, queries, store, sendbuf, kv, v_rows, rec_tiled,
    fresh, part, keep, stack, q_t, m_all, l_all, acc_all,
    load_sem, req_send, req_recv, smem_sem, page_send, page_recv, ctx_send, ctx_recv, hop_send, hop_recv,
    hop_out, spare_out, *landing,
):
    n, ctx_count, kv_heads, slots, pages, page_len, rows, heads, hd = dims
    parts = kv_heads * HALVES
    pieces = parts * 2
    run = page_len // HALVES
    length = pages * run
    group = heads // kv_heads
    columns = group * rows
    pages_all = pages * ctx_count
    recvbuf, hop_in = landing[:pieces], landing[pieces:]
    planes = n // PLANE
    i32 = jnp.int32
    me = lax.axis_index("cache")
    c = lax.axis_index("ctx")

    arrays = (
        (owner_in, owner_row), (slot_in, slot_row), (raw_in, raw),
        (rec_hbm, rec_in), (fresh_in, fresh_raw), (queries_in, queries),
    )
    loads = [pltpu.make_async_copy(src, dst, load_sem.at[i]) for i, (src, dst) in enumerate(arrays)]
    for load in loads:
        load.start()

    barrier = pltpu.get_barrier_semaphore()

    def greet(k, _):
        pl.semaphore_signal(barrier, inc=1, device_id={"cache": lax.rem(me + k, n)}, device_id_type=MESH)
        return 0

    lax.fori_loop(1, n, greet, 0)
    for step in (1, ctx_count - 1):
        pl.semaphore_signal(barrier, inc=1, device_id={"ctx": lax.rem(c + step, ctx_count)}, device_id_type=MESH)

    a = lax.broadcasted_iota(i32, (pages_all, pages_all), 0)
    b = lax.broadcasted_iota(i32, (pages_all, pages_all), 1)
    loads[0].wait()
    loads[1].wait()
    owner = owner_row[...]
    owner_f = jnp.broadcast_to(owner, (pages_all, pages_all)).astype(jnp.float32)
    owner_of_a = jnp.sum(jnp.where(a == b, owner_f, 0.0), axis=1, keepdims=True).astype(i32)
    low = c * pages
    one_block = a // pages == b // pages
    alike = (owner_of_a == owner) & one_block
    second = jnp.max(jnp.where(alike & (a < b), 1, 0), axis=0, keepdims=True)
    if shared:
        second_of_a = jnp.max(jnp.where(alike & (b < a), 1.0, 0.0), axis=1, keepdims=True)
        beside = one_block & (owner_of_a // PLANE == owner // PLANE) & (second_of_a > 0.5)
        lowest = jnp.min(jnp.where(beside, owner_of_a % PLANE, PLANE), axis=0, keepdims=True)
        spare = n + owner // PLANE * SPARE + jnp.where(owner % PLANE == lowest, 0, 1)
        where_to = jnp.where(second > 0, spare, owner)
    else:
        where_to = owner * 2 + second
    idx_rows[...] = jnp.broadcast_to(where_to, idx_rows.shape)
    to_idx = pltpu.make_async_copy(idx_rows, idx, smem_sem.at[0])
    to_idx.start()

    shard = lax.broadcasted_iota(i32, (n, pages_all), 0)
    place_of = lax.broadcasted_iota(i32, (n, pages_all), 1)
    named = (shard == owner) & (place_of >= low) & (place_of < low + pages)
    coded = (place_of * slots + slot_row[...]).astype(jnp.float32)
    first = jnp.min(jnp.where(named, coded, float(pages_all * slots)), axis=1, keepdims=True)
    final = jnp.max(jnp.where(named, coded, 0.0), axis=1, keepdims=True)
    asked = jnp.where(place_of == 0, first, final).astype(i32) % slots
    if shared:
        mine = (shard // PLANE == owner // PLANE) & (second > 0)
        here = mine & (place_of >= low) & (place_of < low + pages)
        member = (owner % PLANE).astype(jnp.float32)
        least = jnp.min(jnp.where(here, member, float(PLANE)), axis=1, keepdims=True).astype(i32) % PLANE
        most = jnp.max(jnp.where(here, member, 0.0), axis=1, keepdims=True).astype(i32) % PLANE
        excess = jnp.zeros((n, 1), jnp.float32)
        for other in range(ctx_count):
            there = mine & (place_of // pages == other)
            excess = jnp.maximum(excess, jnp.sum(jnp.where(there, 1.0, 0.0), axis=1, keepdims=True))
        excess = jnp.max(excess, axis=0, keepdims=True)
        asked = jnp.where(place_of == 2, least, asked)
        asked = jnp.where(place_of == 3, most, asked)
        asked = jnp.where(place_of == 4, jnp.where(excess > SPARE, 1, 0), asked)
    for d in range(n):
        req[d] = asked[d : d + 1, :]

    loads[2].wait()

    def split(p, _):
        store[pl.ds(p * kv_heads, kv_heads)] = jnp.swapaxes(raw[p], 0, 1)
        return 0

    lax.fori_loop(0, slots, split, 0)
    to_idx.wait()
    pl.semaphore_wait(barrier, n + 1)

    def ask(k, _):
        d = lax.rem(me + k, n)
        pltpu.make_async_remote_copy(
            req.at[d], req_in.at[me], req_send, req_recv, device_id={"cache": d}, device_id_type=MESH
        ).start()
        return 0

    lax.fori_loop(1, n, ask, 0)
    req_in[me] = req[me]

    others = req_in.at[pl.ds(0, n - 1)]
    pltpu.make_async_copy(others, others, req_recv).wait()
    to_smem = pltpu.make_async_copy(req_in, req_smem, smem_sem.at[1])
    to_smem.start()
    over[...] = jnp.max(req_in[...], axis=0)
    to_smem.wait()

    def piece_of(q):
        half, which = q // 2 % HALVES, q % 2
        return q // (2 * HALVES), slice(half * run, (half + 1) * run), slice(which * hd, (which + 1) * hd)

    def page(q, d, r):
        k, span, lanes = piece_of(q)
        return store[req_smem[d, 0, r] * kv_heads + k, span, lanes]

    z, m = me // PLANE, me % PLANE

    def mate_copy(q, mate):
        return pltpu.make_async_remote_copy(
            hop_out.at[q, mate], hop_in[q].at[m], hop_send.at[q], hop_recv.at[q],
            device_id={"cache": z * PLANE + mate}, device_id_type=MESH,
        )

    def to_mates(q):
        def fill(i, _):
            for mate in range(PLANE):
                hop_out[q, mate, i] = page(q, i * PLANE + mate, 1)
            hop_in[q][m, i] = page(q, i * PLANE + m, 1)
            return 0

        lax.fori_loop(0, planes, fill, 0)
        for t in range(1, PLANE):
            mate_copy(q, (m + t) % PLANE).start()

    def give_first(q):
        def give(step, _):
            d = lax.rem(me + step, n)
            sendbuf[q, d, 0] = page(q, d, 0)
            pltpu.make_async_remote_copy(
                sendbuf.at[q, d, 0], recvbuf[q].at[me], page_send.at[q], page_recv.at[q],
                device_id={"cache": d}, device_id_type=MESH,
            ).start()
            return 0

        lax.fori_loop(1, n, give, 0)
        recvbuf[q][me] = page(q, me, 0)

    def give_spare(q):
        arrived = hop_in[q].at[pl.ds(0, PLANE - 1)]
        pltpu.make_async_copy(arrived, arrived, hop_recv.at[q]).wait()

        def give(step, _):
            i = lax.rem(z + step, planes)
            d = i * PLANE + m
            for e in range(SPARE):
                spare_out[q, i, e] = hop_in[q][req_smem[d, 0, 2 + e] & (PLANE - 1), i]
            pltpu.make_async_remote_copy(
                spare_out.at[q, i], recvbuf[q].at[pl.ds(n + z * SPARE, SPARE)], page_send.at[q], page_recv.at[q],
                device_id={"cache": d}, device_id_type=MESH,
            ).start()
            return 0

        lax.fori_loop(1, planes, give, 0)
        for e in range(SPARE):
            recvbuf[q][n + z * SPARE + e] = hop_in[q][req_smem[me, 0, 2 + e] & (PLANE - 1), z]

    def give_both(q):
        def give(step, _):
            d = lax.rem(me + step, n)
            for r in range(2):
                sendbuf[q, d, r] = page(q, d, r)
            pltpu.make_async_remote_copy(
                sendbuf.at[q, d], recvbuf[q].at[pl.ds(me * 2, 2)], page_send.at[q], page_recv.at[q],
                device_id={"cache": d}, device_id_type=MESH,
            ).start()
            return 0

        lax.fori_loop(1, n, give, 0)
        for r in range(2):
            recvbuf[q][me * 2 + r] = page(q, me, r)

    def send(q):
        if shared:
            if q < pieces:
                give_first(q)
            if q + LEAD < pieces:
                to_mates(q + LEAD)
            if 0 < q <= pieces:
                give_spare(q - 1)
        elif q < pieces:
            give_both(q)

    if shared:
        for q in range(LEAD):
            to_mates(q)
    for q in range(AHEAD):
        send(q)
    foreign = n - 1 + (planes - 1) * SPARE if shared else 2 * (n - 1)

    loads[3].wait()
    fresh_pos = jnp.zeros((1, rows), i32)
    for other in range(ctx_count):
        theirs = rec_in[:, other * rows : (other + 1) * rows]
        fresh_pos = jnp.where(c == other, theirs, fresh_pos)
    for g in range(group):
        rec_tiled[:, g * rows : (g + 1) * rows] = fresh_pos
    loads[4].wait()
    by_head = jnp.swapaxes(fresh_raw[...], 0, 1)
    for k in range(kv_heads):
        fresh[k] = by_head[k]
    loads[5].wait()
    for half in range(HALVES):
        local = lax.broadcasted_iota(jnp.int32, (length, rows), 0)
        pos = (local // run) * page_len + half * run + local % run
        hit = jnp.where(pos == fresh_pos, 1.0, 0.0)
        covered = jnp.sum(hit, axis=1, keepdims=True)
        keep[half] = jnp.broadcast_to(1.0 - covered, (length, hd)).astype(jnp.bfloat16)
        one_hot = hit.astype(jnp.bfloat16)
        for k in range(kv_heads):
            part[k * HALVES + half] = jnp.dot(
                one_hot, fresh[k], preferred_element_type=jnp.float32
            ).astype(jnp.bfloat16)

    for g in range(heads):
        at = (g % group) * rows
        stack[g // group, at : at + rows, :] = queries[:, g * hd : (g + 1) * hd]
    for k in range(kv_heads):
        for at in range(0, columns, 128):
            block = stack[k, at : at + 128, :].astype(jnp.float32)
            q_t[k, :, at : at + 128] = block.T.astype(jnp.bfloat16)
    m_all[...] = jnp.full(m_all.shape, EMPTY, jnp.float32)
    l_all[...] = jnp.zeros(l_all.shape, jnp.float32)
    acc_all[...] = jnp.zeros(acc_all.shape, jnp.float32)

    factor = hd**-0.5 * math.log2(math.e)

    def attend(q, block, own):
        k = q // HALVES
        at = q * ctx_count + block
        keys = kv[at, :length, :]
        values = jnp.concatenate(
            [kv[at, length + i : length + i + 128, :] for i in range(0, length, 128)], axis=1
        )
        scores = jnp.dot(keys, q_t[k], preferred_element_type=jnp.float32)
        if own:
            local = lax.broadcasted_iota(jnp.int32, (length, 1), 0)
            pos = (local // run) * page_len + (q % HALVES) * run + local % run
            scores = jnp.where(pos <= rec_tiled[...], scores, HIDDEN)
        m_old = m_all[k]
        m_new = jnp.maximum(m_old, jnp.max(scores, axis=0, keepdims=True))
        alpha = jnp.exp2((m_old - m_new) * factor)
        weights = jnp.exp2((scores - m_new[:1]) * factor)
        l_all[k] = l_all[k] * alpha + jnp.sum(weights, axis=0, keepdims=True)
        acc_all[k] = acc_all[k] * alpha[:1] + jnp.dot(
            values, weights.astype(jnp.bfloat16), preferred_element_type=jnp.float32
        )
        m_all[k] = m_new

    def along(q, block, sem, to):
        ref = kv.at[q // 2 * ctx_count + block, pl.ds(q % 2 * length, length)]
        return pltpu.make_async_remote_copy(
            ref, ref, ctx_send.at[q, sem], ctx_recv.at[q, block], device_id={"ctx": to}, device_id_type=MESH
        )

    def finish(k):
        for at in range(0, columns, 128):
            span = slice(at, at + 128)
            stack[k, span, :] = (acc_all[k, :, span] / l_all[k, :1, span]).T.astype(jnp.bfloat16)
        for g in range(group):
            head = k * group + g
            out[:, head * hd : (head + 1) * hd] = stack[k, g * rows : (g + 1) * rows, :]

    for q in range(pieces):
        others = recvbuf[q].at[pl.ds(0, foreign)]
        pltpu.make_async_copy(others, others, page_recv.at[q]).wait()
        k, _, lanes = piece_of(q)
        own_part = q // 2 * ctx_count + c

        def place(j, _, q=q, lanes=lanes, own_part=own_part):
            at = idx[0, c * pages + j]
            spot = pl.ds(pl.multiple_of(j * run, run), run)
            page = recvbuf[q][at] * keep[q // 2 % HALVES, spot, :] + part[q // 2, spot, lanes]
            if q % 2 == 0:
                kv[own_part, spot, :] = page
            else:
                v_rows[spot, :] = page
            return 0

        lax.fori_loop(0, pages, place, 0)
        if q % 2 == 1:
            for i in range(0, length, 128):
                block = v_rows[i : i + 128, :].astype(jnp.float32)
                kv[own_part, length + i : length + i + 128, :] = block.T.astype(jnp.bfloat16)

        @pl.when(c == 0)
        def _(q=q):
            along(q, 0, 1, 3).start()
            along(q, 0, 0, 1).start()

        @pl.when(c == 1)
        def _(q=q):
            if q % 2 == 1:
                along(q, 1, 1, 0).start()
            along(q, 1, 0, 2).start()

        @pl.when(c == 2)
        def _(q=q):
            along(q, 2, 0, 3).start()

        send(q + AHEAD)

        if q % 2 == 0:
            @pl.when(c == 2)
            def _(q=q):
                along(q, 1, 0, 2).wait_recv()
                along(q, 1, 1, 3).start()

            @pl.when(c == 3)
            def _(q=q):
                along(q, 0, 0, 3).wait_recv()
                along(q, 0, 0, 2).start()

            continue

        attend(q // 2, c, True)

        @pl.when(c == 0)
        def _(q=q):
            along(q, 1, 1, 0).wait_recv()
            along(q, 1, 2, 3).start()

        def earlier(t, _, q=q):
            last = c // 3
            block = last * ((3 - t) % 3) + (1 - last) * (c - 1 - t)

            @pl.when((c == 1) | (t > 0))
            def _():
                along(q - 1, block, 0, c).wait_recv()

            along(q, block, 0, c).wait_recv()

            @pl.when((c == 3) & (t == 0))
            def _():
                along(q, 0, 0, 2).start()

            attend(q // 2, block, False)
            return 0

        lax.fori_loop(0, c, earlier, 0)
        if (q + 1) % (2 * HALVES) == 0:
            finish(k)

    pltpu.make_async_copy(req.at[pl.ds(0, n - 1)], req.at[pl.ds(0, n - 1)], req_send).wait()
    for q in range(pieces):
        given = recvbuf[q].at[pl.ds(0, foreign)]
        pltpu.make_async_copy(given, given, page_send.at[q]).wait()
        if shared:
            passed = hop_in[q].at[pl.ds(0, PLANE - 1)]
            pltpu.make_async_copy(passed, passed, hop_send.at[q]).wait()

        @pl.when(c == 0)
        def _(q=q):
            along(q, 0, 0, 1).wait_send()
            along(q, 0, 1, 3).wait_send()
            if q % 2 == 1:
                along(q, 1, 2, 3).wait_send()

        @pl.when(c == 1)
        def _(q=q):
            along(q, 1, 0, 2).wait_send()
            if q % 2 == 1:
                along(q, 1, 1, 0).wait_send()

        @pl.when(c == 2)
        def _(q=q):
            along(q, 2, 0, 3).wait_send()
            if q % 2 == 0:
                along(q, 1, 1, 3).wait_send()

        @pl.when(c == 3)
        def _(q=q):
            along(q, 0, 0, 2).wait_send()


def shards(queries, fresh_kv, kv_store, page_owner, page_slot, rec_index):
    n, ctx_count = lax.axis_size("cache"), lax.axis_size("ctx")
    rows, kv_heads, hd = queries.shape[1], fresh_kv.shape[2], fresh_kv.shape[3] // 2
    heads = queries.shape[2] // hd
    slots, page_len = kv_store.shape[:2]
    pages_all = page_owner.shape[1]
    pages = pages_all // ctx_count
    parts, run = kv_heads * HALVES, page_len // HALVES
    pieces, length = 2 * parts, pages * run
    columns = heads // kv_heads * rows
    dims = (n, ctx_count, kv_heads, slots, pages, page_len, rows, heads, hd)
    bf16, f32, i32 = jnp.bfloat16, jnp.float32, jnp.int32
    vmem, hbm = pl.BlockSpec(memory_space=pltpu.VMEM), pl.BlockSpec(memory_space=pltpu.HBM)
    dma = pltpu.SemaphoreType.DMA
    def call(shared, *arrays):
        return pl.pallas_call(
            functools.partial(kernel, dims, shared),
            out_shape=[jax.ShapeDtypeStruct((rows, heads * hd), bf16), jax.ShapeDtypeStruct((1, 128), i32)],
            in_specs=[hbm] * 6,
            out_specs=[vmem, vmem],
            scratch_shapes=[
                pltpu.VMEM((1, pages_all), i32),
                pltpu.VMEM((1, pages_all), i32),
                pltpu.VMEM(rec_index.shape, i32),
                pltpu.VMEM((n, 1, 128), i32),
                pltpu.VMEM((n, 1, 128), i32),
                pltpu.SMEM((n, 1, 128), i32),
                pltpu.VMEM((8, pages_all), i32),
                pltpu.SMEM((8, pages_all), i32),
                pltpu.VMEM((slots, page_len, kv_heads, 2 * hd), bf16),
                pltpu.VMEM((rows, kv_heads, 2 * hd), bf16),
                pltpu.VMEM((rows, heads * hd), bf16),
                pltpu.VMEM((slots * kv_heads, page_len, 2 * hd), bf16),
                pltpu.VMEM((pieces, n, 2, run, hd), bf16),
                pltpu.VMEM((parts * ctx_count, 2 * length, hd), bf16),
                pltpu.VMEM((length, hd), bf16),
                pltpu.VMEM((1, columns), i32),
                pltpu.VMEM((kv_heads, rows, 2 * hd), bf16),
                pltpu.VMEM((parts, length, 2 * hd), bf16),
                pltpu.VMEM((HALVES, length, hd), bf16),
                pltpu.VMEM((kv_heads, columns, hd), bf16),
                pltpu.VMEM((kv_heads, hd, columns), bf16),
                pltpu.VMEM((kv_heads, 8, columns), f32),
                pltpu.VMEM((kv_heads, 8, columns), f32),
                pltpu.VMEM((kv_heads, hd, columns), f32),
                dma((6,)), dma, dma, dma((2,)),
                dma((pieces,)), dma((pieces,)),
                dma((pieces, 3)), dma((pieces, ctx_count)),
                dma((pieces,)), dma((pieces,)),
                pltpu.VMEM((pieces, PLANE, n // PLANE, run, hd), bf16),
                pltpu.VMEM((pieces, n // PLANE, SPARE, run, hd), bf16),
                *[pltpu.VMEM((2 * n, run, hd), bf16) for _ in range(pieces)],
                *[pltpu.VMEM((PLANE, n // PLANE, run, hd), bf16) for _ in range(pieces)],
            ],
            compiler_params=pltpu.CompilerParams(
                collective_id=0 if shared else 1, has_side_effects=True, vmem_limit_bytes=60 * 1024 * 1024
            ),
        )(*arrays)

    arrays = (page_owner[:, :, 0], page_slot, rec_index, kv_store, fresh_kv[0], queries[0])
    result, over = call(True, *arrays)
    result = lax.cond(over[0, 4] > 0, lambda: call(False, *arrays)[0], lambda: result)
    return result[None]


def solution(mesh):
    in_specs = (
        P("cache", "ctx", "head"),
        P("cache", "ctx", "head", None),
        P("cache", None, "head", None),
        P("cache", None, None),
        P("cache", None),
        P("cache", None),
    )
    out_specs = P("cache", "ctx", "head")
    return jax.shard_map(shards, mesh=mesh, in_specs=in_specs, out_specs=out_specs, check_vma=False)
```

```python
import functools
import math

import jax
import jax.numpy as jnp
from jax import lax
from jax.experimental import pallas as pl
from jax.experimental.pallas import tpu as pltpu
from jax.sharding import PartitionSpec as P

MESH = pl.DeviceIdType.MESH
EMPTY = -1e30
HIDDEN = -2e30
HALVES = 2
AHEAD = 3
LEAD = 2
PLANE = 4
SPARE = 2


def kernel(
    dims, shared, owner_in, slot_in, rec_hbm, raw_in, fresh_in, queries_in, out, over,
    owner_row, slot_row, rec_in, req, req_in, req_smem, idx_rows, idx, raw, fresh_raw, queries, store, sendbuf, kv, v_rows, rec_tiled,
    fresh, part, keep, stack, q_t, m_all, l_all, acc_all,
    load_sem, req_send, req_recv, smem_sem, page_send, page_recv, ctx_send, ctx_recv, hop_send, hop_recv,
    hop_out, spare_out, *landing,
):
    n, ctx_count, kv_heads, slots, pages, page_len, rows, heads, hd = dims
    parts = kv_heads * HALVES
    pieces = parts * 2
    run = page_len // HALVES
    length = pages * run
    group = heads // kv_heads
    columns = group * rows
    pages_all = pages * ctx_count
    recvbuf, hop_in = landing[:pieces], landing[pieces:]
    planes = n // PLANE
    i32 = jnp.int32
    me = lax.axis_index("cache")
    c = lax.axis_index("ctx")

    arrays = (
        (owner_in, owner_row), (slot_in, slot_row), (raw_in, raw),
        (rec_hbm, rec_in), (fresh_in, fresh_raw), (queries_in, queries),
    )
    loads = [pltpu.make_async_copy(src, dst, load_sem.at[i]) for i, (src, dst) in enumerate(arrays)]
    for load in loads:
        load.start()

    barrier = pltpu.get_barrier_semaphore()

    def greet(k, _):
        pl.semaphore_signal(barrier, inc=1, device_id={"cache": lax.rem(me + k, n)}, device_id_type=MESH)
        return 0

    lax.fori_loop(1, n, greet, 0)
    for step in (1, ctx_count - 1):
        pl.semaphore_signal(barrier, inc=1, device_id={"ctx": lax.rem(c + step, ctx_count)}, device_id_type=MESH)

    a = lax.broadcasted_iota(i32, (pages_all, pages_all), 0)
    b = lax.broadcasted_iota(i32, (pages_all, pages_all), 1)
    loads[0].wait()
    loads[1].wait()
    owner = owner_row[...]
    owner_f = jnp.broadcast_to(owner, (pages_all, pages_all)).astype(jnp.float32)
    owner_of_a = jnp.sum(jnp.where(a == b, owner_f, 0.0), axis=1, keepdims=True).astype(i32)
    low = c * pages
    one_block = a // pages == b // pages
    alike = (owner_of_a == owner) & one_block
    second = jnp.max(jnp.where(alike & (a < b), 1, 0), axis=0, keepdims=True)
    if shared:
        second_of_a = jnp.max(jnp.where(alike & (b < a), 1.0, 0.0), axis=1, keepdims=True)
        beside = one_block & (owner_of_a // PLANE == owner // PLANE) & (second_of_a > 0.5)
        lowest = jnp.min(jnp.where(beside, owner_of_a % PLANE, PLANE), axis=0, keepdims=True)
        spare = n + owner // PLANE * SPARE + jnp.where(owner % PLANE == lowest, 0, 1)
        where_to = jnp.where(second > 0, spare, owner)
    else:
        where_to = owner * 2 + second
    idx_rows[...] = jnp.broadcast_to(where_to, idx_rows.shape)
    to_idx = pltpu.make_async_copy(idx_rows, idx, smem_sem.at[0])
    to_idx.start()

    shard = lax.broadcasted_iota(i32, (n, pages_all), 0)
    place_of = lax.broadcasted_iota(i32, (n, pages_all), 1)
    named = (shard == owner) & (place_of >= low) & (place_of < low + pages)
    coded = (place_of * slots + slot_row[...]).astype(jnp.float32)
    first = jnp.min(jnp.where(named, coded, float(pages_all * slots)), axis=1, keepdims=True)
    final = jnp.max(jnp.where(named, coded, 0.0), axis=1, keepdims=True)
    asked = jnp.where(place_of == 0, first, final).astype(i32) % slots
    if shared:
        mine = (shard // PLANE == owner // PLANE) & (second > 0)
        here = mine & (place_of >= low) & (place_of < low + pages)
        member = (owner % PLANE).astype(jnp.float32)
        least = jnp.min(jnp.where(here, member, float(PLANE)), axis=1, keepdims=True).astype(i32) % PLANE
        most = jnp.max(jnp.where(here, member, 0.0), axis=1, keepdims=True).astype(i32) % PLANE
        excess = jnp.zeros((n, 1), jnp.float32)
        for other in range(ctx_count):
            there = mine & (place_of // pages == other)
            excess = jnp.maximum(excess, jnp.sum(jnp.where(there, 1.0, 0.0), axis=1, keepdims=True))
        excess = jnp.max(excess, axis=0, keepdims=True)
        asked = jnp.where(place_of == 2, least, asked)
        asked = jnp.where(place_of == 3, most, asked)
        asked = jnp.where(place_of == 4, jnp.where(excess > SPARE, 1, 0), asked)
    for d in range(n):
        req[d] = asked[d : d + 1, :]

    loads[2].wait()

    def split(p, _):
        store[pl.ds(p * kv_heads, kv_heads)] = jnp.swapaxes(raw[p], 0, 1)
        return 0

    lax.fori_loop(0, slots, split, 0)
    to_idx.wait()
    pl.semaphore_wait(barrier, n + 1)

    def ask(k, _):
        d = lax.rem(me + k, n)
        pltpu.make_async_remote_copy(
            req.at[d], req_in.at[me], req_send, req_recv, device_id={"cache": d}, device_id_type=MESH
        ).start()
        return 0

    lax.fori_loop(1, n, ask, 0)
    req_in[me] = req[me]

    others = req_in.at[pl.ds(0, n - 1)]
    pltpu.make_async_copy(others, others, req_recv).wait()
    to_smem = pltpu.make_async_copy(req_in, req_smem, smem_sem.at[1])
    to_smem.start()
    over[...] = jnp.max(req_in[...], axis=0)
    to_smem.wait()

    def piece_of(q):
        half, which = q // 2 % HALVES, q % 2
        return q // (2 * HALVES), slice(half * run, (half + 1) * run), slice(which * hd, (which + 1) * hd)

    def page(q, d, r):
        k, span, lanes = piece_of(q)
        return store[req_smem[d, 0, r] * kv_heads + k, span, lanes]

    z, m = me // PLANE, me % PLANE

    def mate_copy(q, mate):
        return pltpu.make_async_remote_copy(
            hop_out.at[q, mate], hop_in[q].at[m], hop_send.at[q], hop_recv.at[q],
            device_id={"cache": z * PLANE + mate}, device_id_type=MESH,
        )

    def to_mates(q):
        def fill(i, _):
            for mate in range(PLANE):
                hop_out[q, mate, i] = page(q, i * PLANE + mate, 1)
            hop_in[q][m, i] = page(q, i * PLANE + m, 1)
            return 0

        lax.fori_loop(0, planes, fill, 0)
        for t in range(1, PLANE):
            mate_copy(q, (m + t) % PLANE).start()

    def give_first(q):
        def give(step, _):
            d = lax.rem(me + step, n)
            sendbuf[q, d, 0] = page(q, d, 0)
            pltpu.make_async_remote_copy(
                sendbuf.at[q, d, 0], recvbuf[q].at[me], page_send.at[q], page_recv.at[q],
                device_id={"cache": d}, device_id_type=MESH,
            ).start()
            return 0

        lax.fori_loop(1, n, give, 0)
        recvbuf[q][me] = page(q, me, 0)

    def give_spare(q):
        arrived = hop_in[q].at[pl.ds(0, PLANE - 1)]
        pltpu.make_async_copy(arrived, arrived, hop_recv.at[q]).wait()

        def give(step, _):
            i = lax.rem(z + step, planes)
            d = i * PLANE + m
            for e in range(SPARE):
                spare_out[q, i, e] = hop_in[q][req_smem[d, 0, 2 + e] & (PLANE - 1), i]
            pltpu.make_async_remote_copy(
                spare_out.at[q, i], recvbuf[q].at[pl.ds(n + z * SPARE, SPARE)], page_send.at[q], page_recv.at[q],
                device_id={"cache": d}, device_id_type=MESH,
            ).start()
            return 0

        lax.fori_loop(1, planes, give, 0)
        for e in range(SPARE):
            recvbuf[q][n + z * SPARE + e] = hop_in[q][req_smem[me, 0, 2 + e] & (PLANE - 1), z]

    def give_both(q):
        def give(step, _):
            d = lax.rem(me + step, n)
            for r in range(2):
                sendbuf[q, d, r] = page(q, d, r)
            pltpu.make_async_remote_copy(
                sendbuf.at[q, d], recvbuf[q].at[pl.ds(me * 2, 2)], page_send.at[q], page_recv.at[q],
                device_id={"cache": d}, device_id_type=MESH,
            ).start()
            return 0

        lax.fori_loop(1, n, give, 0)
        for r in range(2):
            recvbuf[q][me * 2 + r] = page(q, me, r)

    def send(q):
        if shared:
            if q < pieces:
                give_first(q)
            if q + LEAD < pieces:
                to_mates(q + LEAD)
            if 0 < q <= pieces:
                give_spare(q - 1)
        elif q < pieces:
            give_both(q)

    if shared:
        for q in range(LEAD):
            to_mates(q)
    for q in range(AHEAD):
        send(q)
    foreign = n - 1 + (planes - 1) * SPARE if shared else 2 * (n - 1)

    loads[3].wait()
    fresh_pos = jnp.zeros((1, rows), i32)
    for other in range(ctx_count):
        theirs = rec_in[:, other * rows : (other + 1) * rows]
        fresh_pos = jnp.where(c == other, theirs, fresh_pos)
    for g in range(group):
        rec_tiled[:, g * rows : (g + 1) * rows] = fresh_pos
    loads[4].wait()
    by_head = jnp.swapaxes(fresh_raw[...], 0, 1)
    for k in range(kv_heads):
        fresh[k] = by_head[k]
    loads[5].wait()
    for half in range(HALVES):
        local = lax.broadcasted_iota(jnp.int32, (length, rows), 0)
        pos = (local // run) * page_len + half * run + local % run
        hit = jnp.where(pos == fresh_pos, 1.0, 0.0)
        covered = jnp.sum(hit, axis=1, keepdims=True)
        keep[half] = jnp.broadcast_to(1.0 - covered, (length, hd)).astype(jnp.bfloat16)
        one_hot = hit.astype(jnp.bfloat16)
        for k in range(kv_heads):
            part[k * HALVES + half] = jnp.dot(
                one_hot, fresh[k], preferred_element_type=jnp.float32
            ).astype(jnp.bfloat16)

    for g in range(heads):
        at = (g % group) * rows
        stack[g // group, at : at + rows, :] = queries[:, g * hd : (g + 1) * hd]
    for k in range(kv_heads):
        for at in range(0, columns, 128):
            block = stack[k, at : at + 128, :].astype(jnp.float32)
            q_t[k, :, at : at + 128] = block.T.astype(jnp.bfloat16)
    m_all[...] = jnp.full(m_all.shape, EMPTY, jnp.float32)
    l_all[...] = jnp.zeros(l_all.shape, jnp.float32)
    acc_all[...] = jnp.zeros(acc_all.shape, jnp.float32)

    factor = hd**-0.5 * math.log2(math.e)

    def attend(q, block, own):
        k = q // HALVES
        at = q * ctx_count + block
        keys = kv[at, :length, :]
        values = jnp.concatenate(
            [kv[at, length + i : length + i + 128, :] for i in range(0, length, 128)], axis=1
        )
        scores = jnp.dot(keys, q_t[k], preferred_element_type=jnp.float32)
        if own:
            local = lax.broadcasted_iota(jnp.int32, (length, 1), 0)
            pos = (local // run) * page_len + (q % HALVES) * run + local % run
            scores = jnp.where(pos <= rec_tiled[...], scores, HIDDEN)
        m_old = m_all[k]
        m_new = jnp.maximum(m_old, jnp.max(scores, axis=0, keepdims=True))
        alpha = jnp.exp2((m_old - m_new) * factor)
        weights = jnp.exp2((scores - m_new[:1]) * factor)
        l_all[k] = l_all[k] * alpha + jnp.sum(weights, axis=0, keepdims=True)
        acc_all[k] = acc_all[k] * alpha[:1] + jnp.dot(
            values, weights.astype(jnp.bfloat16), preferred_element_type=jnp.float32
        )
        m_all[k] = m_new

    def along(q, block, sem, to):
        ref = kv.at[q // 2 * ctx_count + block, pl.ds(q % 2 * length, length)]
        return pltpu.make_async_remote_copy(
            ref, ref, ctx_send.at[q, sem], ctx_recv.at[q, block], device_id={"ctx": to}, device_id_type=MESH
        )

    def finish(k):
        for at in range(0, columns, 128):
            span = slice(at, at + 128)
            stack[k, span, :] = (acc_all[k, :, span] / l_all[k, :1, span]).T.astype(jnp.bfloat16)
        for g in range(group):
            head = k * group + g
            out[:, head * hd : (head + 1) * hd] = stack[k, g * rows : (g + 1) * rows, :]

    def forward(q):
        if q % 2 == 0:

            @pl.when(c == 2)
            def _():
                along(q, 1, 0, 2).wait_recv()
                along(q, 1, 1, 3).start()

        else:

            @pl.when(c == 0)
            def _():
                along(q, 1, 1, 0).wait_recv()
                along(q, 1, 2, 3).start()

        @pl.when(c == 3)
        def _():
            along(q, 0, 0, 3).wait_recv()
            along(q, 0, 0, 2).start()

    def fold_earlier(p):
        def earlier(t, _):
            last = c // 3
            block = last * ((3 - t) % 3) + (1 - last) * (c - 1 - t)

            @pl.when((c == 1) | (t > 0))
            def _():
                along(2 * p, block, 0, c).wait_recv()

            @pl.when((c < 3) | (t > 0))
            def _():
                along(2 * p + 1, block, 0, c).wait_recv()

            attend(p, block, False)
            return 0

        lax.fori_loop(0, c, earlier, 0)
        if (p + 1) % HALVES == 0:
            finish(p // HALVES)

    for q in range(pieces):
        others = recvbuf[q].at[pl.ds(0, foreign)]
        pltpu.make_async_copy(others, others, page_recv.at[q]).wait()
        k, _, lanes = piece_of(q)
        own_part = q // 2 * ctx_count + c

        def place(j, _, q=q, lanes=lanes, own_part=own_part):
            at = idx[0, c * pages + j]
            spot = pl.ds(pl.multiple_of(j * run, run), run)
            page = recvbuf[q][at] * keep[q // 2 % HALVES, spot, :] + part[q // 2, spot, lanes]
            if q % 2 == 0:
                kv[own_part, spot, :] = page
            else:
                v_rows[spot, :] = page
            return 0

        lax.fori_loop(0, pages, place, 0)
        if q % 2 == 1:
            for i in range(0, length, 128):
                block = v_rows[i : i + 128, :].astype(jnp.float32)
                kv[own_part, length + i : length + i + 128, :] = block.T.astype(jnp.bfloat16)

        @pl.when(c == 0)
        def _(q=q):
            along(q, 0, 1, 3).start()
            along(q, 0, 0, 1).start()

        @pl.when(c == 1)
        def _(q=q):
            if q % 2 == 1:
                along(q, 1, 1, 0).start()
            along(q, 1, 0, 2).start()

        @pl.when(c == 2)
        def _(q=q):
            along(q, 2, 0, 3).start()

        send(q + AHEAD)

        if 0 < q < pieces - 1:
            forward(q - 1)
        if q % 2 == 1:
            attend(q // 2, c, True)
        elif q > 0:
            fold_earlier(q // 2 - 1)
        if q == pieces - 2:
            forward(q)
    forward(pieces - 1)
    fold_earlier(parts - 1)

    pltpu.make_async_copy(req.at[pl.ds(0, n - 1)], req.at[pl.ds(0, n - 1)], req_send).wait()
    for q in range(pieces):
        given = recvbuf[q].at[pl.ds(0, foreign)]
        pltpu.make_async_copy(given, given, page_send.at[q]).wait()
        if shared:
            passed = hop_in[q].at[pl.ds(0, PLANE - 1)]
            pltpu.make_async_copy(passed, passed, hop_send.at[q]).wait()

        @pl.when(c == 0)
        def _(q=q):
            along(q, 0, 0, 1).wait_send()
            along(q, 0, 1, 3).wait_send()
            if q % 2 == 1:
                along(q, 1, 2, 3).wait_send()

        @pl.when(c == 1)
        def _(q=q):
            along(q, 1, 0, 2).wait_send()
            if q % 2 == 1:
                along(q, 1, 1, 0).wait_send()

        @pl.when(c == 2)
        def _(q=q):
            along(q, 2, 0, 3).wait_send()
            if q % 2 == 0:
                along(q, 1, 1, 3).wait_send()

        @pl.when(c == 3)
        def _(q=q):
            along(q, 0, 0, 2).wait_send()


def shards(queries, fresh_kv, kv_store, page_owner, page_slot, rec_index):
    n, ctx_count = lax.axis_size("cache"), lax.axis_size("ctx")
    rows, kv_heads, hd = queries.shape[1], fresh_kv.shape[2], fresh_kv.shape[3] // 2
    heads = queries.shape[2] // hd
    slots, page_len = kv_store.shape[:2]
    pages_all = page_owner.shape[1]
    pages = pages_all // ctx_count
    parts, run = kv_heads * HALVES, page_len // HALVES
    pieces, length = 2 * parts, pages * run
    columns = heads // kv_heads * rows
    dims = (n, ctx_count, kv_heads, slots, pages, page_len, rows, heads, hd)
    bf16, f32, i32 = jnp.bfloat16, jnp.float32, jnp.int32
    vmem, hbm = pl.BlockSpec(memory_space=pltpu.VMEM), pl.BlockSpec(memory_space=pltpu.HBM)
    dma = pltpu.SemaphoreType.DMA
    def call(shared, *arrays):
        return pl.pallas_call(
            functools.partial(kernel, dims, shared),
            out_shape=[jax.ShapeDtypeStruct((rows, heads * hd), bf16), jax.ShapeDtypeStruct((1, 128), i32)],
            in_specs=[hbm] * 6,
            out_specs=[vmem, vmem],
            scratch_shapes=[
                pltpu.VMEM((1, pages_all), i32),
                pltpu.VMEM((1, pages_all), i32),
                pltpu.VMEM(rec_index.shape, i32),
                pltpu.VMEM((n, 1, 128), i32),
                pltpu.VMEM((n, 1, 128), i32),
                pltpu.SMEM((n, 1, 128), i32),
                pltpu.VMEM((8, pages_all), i32),
                pltpu.SMEM((8, pages_all), i32),
                pltpu.VMEM((slots, page_len, kv_heads, 2 * hd), bf16),
                pltpu.VMEM((rows, kv_heads, 2 * hd), bf16),
                pltpu.VMEM((rows, heads * hd), bf16),
                pltpu.VMEM((slots * kv_heads, page_len, 2 * hd), bf16),
                pltpu.VMEM((pieces, n, 2, run, hd), bf16),
                pltpu.VMEM((parts * ctx_count, 2 * length, hd), bf16),
                pltpu.VMEM((length, hd), bf16),
                pltpu.VMEM((1, columns), i32),
                pltpu.VMEM((kv_heads, rows, 2 * hd), bf16),
                pltpu.VMEM((parts, length, 2 * hd), bf16),
                pltpu.VMEM((HALVES, length, hd), bf16),
                pltpu.VMEM((kv_heads, columns, hd), bf16),
                pltpu.VMEM((kv_heads, hd, columns), bf16),
                pltpu.VMEM((kv_heads, 8, columns), f32),
                pltpu.VMEM((kv_heads, 8, columns), f32),
                pltpu.VMEM((kv_heads, hd, columns), f32),
                dma((6,)), dma, dma, dma((2,)),
                dma((pieces,)), dma((pieces,)),
                dma((pieces, 3)), dma((pieces, ctx_count)),
                dma((pieces,)), dma((pieces,)),
                pltpu.VMEM((pieces, PLANE, n // PLANE, run, hd), bf16),
                pltpu.VMEM((pieces, n // PLANE, SPARE, run, hd), bf16),
                *[pltpu.VMEM((2 * n, run, hd), bf16) for _ in range(pieces)],
                *[pltpu.VMEM((PLANE, n // PLANE, run, hd), bf16) for _ in range(pieces)],
            ],
            compiler_params=pltpu.CompilerParams(
                collective_id=0 if shared else 1, has_side_effects=True, vmem_limit_bytes=60 * 1024 * 1024
            ),
        )(*arrays)

    arrays = (page_owner[:, :, 0], page_slot, rec_index, kv_store, fresh_kv[0], queries[0])
    result, over = call(True, *arrays)
    result = lax.cond(over[0, 4] > 0, lambda: call(False, *arrays)[0], lambda: result)
    return result[None]


def solution(mesh):
    in_specs = (
        P("cache", "ctx", "head"),
        P("cache", "ctx", "head", None),
        P("cache", None, "head", None),
        P("cache", None, None),
        P("cache", None),
        P("cache", None),
    )
    out_specs = P("cache", "ctx", "head")
    return jax.shard_map(shards, mesh=mesh, in_specs=in_specs, out_specs=out_specs, check_vma=False)
```

```python
import functools
import math

import jax
import jax.numpy as jnp
from jax import lax
from jax.experimental import pallas as pl
from jax.experimental.pallas import tpu as pltpu
from jax.sharding import PartitionSpec as P

MESH = pl.DeviceIdType.MESH
EMPTY = -1e30
HIDDEN = -2e30
HALVES = 2
AHEAD = 3
LEAD = 2
PLANE = 4
SPARE = 2


def kernel(
    dims, shared, owner_in, slot_in, rec_hbm, raw_in, fresh_in, queries_in, out, over,
    owner_row, slot_row, rec_in, req, req_in, req_smem, idx_rows, idx, raw, fresh_raw, queries, store, sendbuf, kv, v_rows, rec_tiled,
    fresh, part, keep, stack, q_t, m_all, l_all, acc_all,
    load_sem, req_send, req_recv, smem_sem, page_send, page_recv, ctx_send, ctx_recv, hop_send, hop_recv,
    hop_out, spare_out, *landing,
):
    n, ctx_count, kv_heads, slots, pages, page_len, rows, heads, hd = dims
    parts = kv_heads * HALVES
    pieces = parts * 2
    run = page_len // HALVES
    length = pages * run
    group = heads // kv_heads
    columns = group * rows
    pages_all = pages * ctx_count
    recvbuf, hop_in = landing[:pieces], landing[pieces:]
    planes = n // PLANE
    i32 = jnp.int32
    me = lax.axis_index("cache")
    c = lax.axis_index("ctx")

    arrays = (
        (owner_in, owner_row), (slot_in, slot_row), (raw_in, raw),
        (rec_hbm, rec_in), (fresh_in, fresh_raw), (queries_in, queries),
    )
    loads = [pltpu.make_async_copy(src, dst, load_sem.at[i]) for i, (src, dst) in enumerate(arrays)]
    for load in loads:
        load.start()

    barrier = pltpu.get_barrier_semaphore()

    def greet(k, _):
        pl.semaphore_signal(barrier, inc=1, device_id={"cache": lax.rem(me + k, n)}, device_id_type=MESH)
        return 0

    lax.fori_loop(1, n, greet, 0)
    for step in (1, ctx_count - 1):
        pl.semaphore_signal(barrier, inc=1, device_id={"ctx": lax.rem(c + step, ctx_count)}, device_id_type=MESH)

    a = lax.broadcasted_iota(i32, (pages_all, pages_all), 0)
    b = lax.broadcasted_iota(i32, (pages_all, pages_all), 1)
    loads[0].wait()
    loads[1].wait()
    owner = owner_row[...]
    owner_f = jnp.broadcast_to(owner, (pages_all, pages_all)).astype(jnp.float32)
    owner_of_a = jnp.sum(jnp.where(a == b, owner_f, 0.0), axis=1, keepdims=True).astype(i32)
    low = c * pages
    one_block = a // pages == b // pages
    alike = (owner_of_a == owner) & one_block
    second = jnp.max(jnp.where(alike & (a < b), 1, 0), axis=0, keepdims=True)
    if shared:
        second_of_a = jnp.max(jnp.where(alike & (b < a), 1.0, 0.0), axis=1, keepdims=True)
        beside = one_block & (owner_of_a // PLANE == owner // PLANE) & (second_of_a > 0.5)
        lowest = jnp.min(jnp.where(beside, owner_of_a % PLANE, PLANE), axis=0, keepdims=True)
        spare = n + owner // PLANE * SPARE + jnp.where(owner % PLANE == lowest, 0, 1)
        where_to = jnp.where(second > 0, spare, owner)
    else:
        where_to = owner * 2 + second
    idx_rows[...] = jnp.broadcast_to(where_to, idx_rows.shape)
    to_idx = pltpu.make_async_copy(idx_rows, idx, smem_sem.at[0])
    to_idx.start()

    shard = lax.broadcasted_iota(i32, (n, pages_all), 0)
    place_of = lax.broadcasted_iota(i32, (n, pages_all), 1)
    named = (shard == owner) & (place_of >= low) & (place_of < low + pages)
    coded = (place_of * slots + slot_row[...]).astype(jnp.float32)
    first = jnp.min(jnp.where(named, coded, float(pages_all * slots)), axis=1, keepdims=True)
    final = jnp.max(jnp.where(named, coded, 0.0), axis=1, keepdims=True)
    asked = jnp.where(place_of == 0, first, final).astype(i32) % slots
    if shared:
        mine = (shard // PLANE == owner // PLANE) & (second > 0)
        here = mine & (place_of >= low) & (place_of < low + pages)
        member = (owner % PLANE).astype(jnp.float32)
        least = jnp.min(jnp.where(here, member, float(PLANE)), axis=1, keepdims=True).astype(i32) % PLANE
        most = jnp.max(jnp.where(here, member, 0.0), axis=1, keepdims=True).astype(i32) % PLANE
        excess = jnp.zeros((n, 1), jnp.float32)
        for other in range(ctx_count):
            there = mine & (place_of // pages == other)
            excess = jnp.maximum(excess, jnp.sum(jnp.where(there, 1.0, 0.0), axis=1, keepdims=True))
        excess = jnp.max(excess, axis=0, keepdims=True)
        asked = jnp.where(place_of == 2, least, asked)
        asked = jnp.where(place_of == 3, most, asked)
        asked = jnp.where(place_of >= 4, jnp.where(excess > SPARE, 1, 0), asked)
    for d in range(n):
        req[d] = asked[d : d + 1, :]

    loads[2].wait()

    def split(p, _):
        store[pl.ds(p * kv_heads, kv_heads)] = jnp.swapaxes(raw[p], 0, 1)
        return 0

    lax.fori_loop(0, slots, split, 0)
    to_idx.wait()
    pl.semaphore_wait(barrier, n + 1)

    def ask(k, _):
        d = lax.rem(me + k, n)
        pltpu.make_async_remote_copy(
            req.at[d], req_in.at[me], req_send, req_recv, device_id={"cache": d}, device_id_type=MESH
        ).start()
        return 0

    lax.fori_loop(1, n, ask, 0)
    req_in[me] = req[me]

    others = req_in.at[pl.ds(0, n - 1)]
    pltpu.make_async_copy(others, others, req_recv).wait()
    to_smem = pltpu.make_async_copy(req_in, req_smem, smem_sem.at[1])
    to_smem.start()
    flags = jnp.max(req_in[...], axis=0).astype(jnp.float32)
    over[...] = jnp.max(flags[:, 4:], axis=1, keepdims=True).astype(i32)
    to_smem.wait()

    def piece_of(q):
        half, which = q // 2 % HALVES, q % 2
        return q // (2 * HALVES), slice(half * run, (half + 1) * run), slice(which * hd, (which + 1) * hd)

    def page(q, d, r):
        k, span, lanes = piece_of(q)
        return store[req_smem[d, 0, r] * kv_heads + k, span, lanes]

    z, m = me // PLANE, me % PLANE

    def mate_copy(q, mate):
        return pltpu.make_async_remote_copy(
            hop_out.at[q, mate], hop_in[q].at[m], hop_send.at[q], hop_recv.at[q],
            device_id={"cache": z * PLANE + mate}, device_id_type=MESH,
        )

    def to_mates(q):
        def fill(i, _):
            for mate in range(PLANE):
                hop_out[q, mate, i] = page(q, i * PLANE + mate, 1)
            hop_in[q][m, i] = page(q, i * PLANE + m, 1)
            return 0

        lax.fori_loop(0, planes, fill, 0)
        for t in range(1, PLANE):
            mate_copy(q, (m + t) % PLANE).start()

    def give_first(q):
        def give(step, _):
            d = lax.rem(me + step, n)
            sendbuf[q, d, 0] = page(q, d, 0)
            pltpu.make_async_remote_copy(
                sendbuf.at[q, d, 0], recvbuf[q].at[me], page_send.at[q], page_recv.at[q],
                device_id={"cache": d}, device_id_type=MESH,
            ).start()
            return 0

        lax.fori_loop(1, n, give, 0)
        recvbuf[q][me] = page(q, me, 0)

    def give_spare(q):
        arrived = hop_in[q].at[pl.ds(0, PLANE - 1)]
        pltpu.make_async_copy(arrived, arrived, hop_recv.at[q]).wait()

        def give(step, _):
            i = lax.rem(z + step, planes)
            d = i * PLANE + m
            for e in range(SPARE):
                spare_out[q, i, e] = hop_in[q][req_smem[d, 0, 2 + e] & (PLANE - 1), i]
            pltpu.make_async_remote_copy(
                spare_out.at[q, i], recvbuf[q].at[pl.ds(n + z * SPARE, SPARE)], page_send.at[q], page_recv.at[q],
                device_id={"cache": d}, device_id_type=MESH,
            ).start()
            return 0

        lax.fori_loop(1, planes, give, 0)
        for e in range(SPARE):
            recvbuf[q][n + z * SPARE + e] = hop_in[q][req_smem[me, 0, 2 + e] & (PLANE - 1), z]

    def give_both(q):
        def give(step, _):
            d = lax.rem(me + step, n)
            for r in range(2):
                sendbuf[q, d, r] = page(q, d, r)
            pltpu.make_async_remote_copy(
                sendbuf.at[q, d], recvbuf[q].at[pl.ds(me * 2, 2)], page_send.at[q], page_recv.at[q],
                device_id={"cache": d}, device_id_type=MESH,
            ).start()
            return 0

        lax.fori_loop(1, n, give, 0)
        for r in range(2):
            recvbuf[q][me * 2 + r] = page(q, me, r)

    def send(q):
        if shared:
            if q < pieces:
                give_first(q)
            if q + LEAD < pieces:
                to_mates(q + LEAD)
            if 0 < q <= pieces:
                give_spare(q - 1)
        elif q < pieces:
            give_both(q)

    if shared:
        for q in range(LEAD):
            to_mates(q)
    for q in range(AHEAD):
        send(q)
    foreign = n - 1 + (planes - 1) * SPARE if shared else 2 * (n - 1)

    loads[3].wait()
    fresh_pos = jnp.zeros((1, rows), i32)
    for other in range(ctx_count):
        theirs = rec_in[:, other * rows : (other + 1) * rows]
        fresh_pos = jnp.where(c == other, theirs, fresh_pos)
    for g in range(group):
        rec_tiled[:, g * rows : (g + 1) * rows] = fresh_pos
    loads[4].wait()
    by_head = jnp.swapaxes(fresh_raw[...], 0, 1)
    for k in range(kv_heads):
        fresh[k] = by_head[k]
    loads[5].wait()
    for half in range(HALVES):
        local = lax.broadcasted_iota(jnp.int32, (length, rows), 0)
        pos = (local // run) * page_len + half * run + local % run
        hit = jnp.where(pos == fresh_pos, 1.0, 0.0)
        covered = jnp.sum(hit, axis=1, keepdims=True)
        keep[half] = jnp.broadcast_to(1.0 - covered, (length, hd)).astype(jnp.bfloat16)
        one_hot = hit.astype(jnp.bfloat16)
        for k in range(kv_heads):
            part[k * HALVES + half] = jnp.dot(
                one_hot, fresh[k], preferred_element_type=jnp.float32
            ).astype(jnp.bfloat16)

    for g in range(heads):
        at = (g % group) * rows
        stack[g // group, at : at + rows, :] = queries[:, g * hd : (g + 1) * hd]
    for k in range(kv_heads):
        for at in range(0, columns, 128):
            block = stack[k, at : at + 128, :].astype(jnp.float32)
            q_t[k, :, at : at + 128] = block.T.astype(jnp.bfloat16)
    m_all[...] = jnp.full(m_all.shape, EMPTY, jnp.float32)
    l_all[...] = jnp.zeros(l_all.shape, jnp.float32)
    acc_all[...] = jnp.zeros(acc_all.shape, jnp.float32)

    factor = hd**-0.5 * math.log2(math.e)

    def attend(q, block, own):
        k = q // HALVES
        at = q * ctx_count + block
        keys = kv[at, :length, :]
        values = jnp.concatenate(
            [kv[at, length + i : length + i + 128, :] for i in range(0, length, 128)], axis=1
        )
        scores = jnp.dot(keys, q_t[k], preferred_element_type=jnp.float32)
        if own:
            local = lax.broadcasted_iota(jnp.int32, (length, 1), 0)
            pos = (local // run) * page_len + (q % HALVES) * run + local % run
            scores = jnp.where(pos <= rec_tiled[...], scores, HIDDEN)
        m_old = m_all[k]
        m_new = jnp.maximum(m_old, jnp.max(scores, axis=0, keepdims=True))
        alpha = jnp.exp2((m_old - m_new) * factor)
        weights = jnp.exp2((scores - m_new[:1]) * factor)
        l_all[k] = l_all[k] * alpha + jnp.sum(weights, axis=0, keepdims=True)
        acc_all[k] = acc_all[k] * alpha[:1] + jnp.dot(
            values, weights.astype(jnp.bfloat16), preferred_element_type=jnp.float32
        )
        m_all[k] = m_new

    def along(q, block, sem, to):
        ref = kv.at[q // 2 * ctx_count + block, pl.ds(q % 2 * length, length)]
        return pltpu.make_async_remote_copy(
            ref, ref, ctx_send.at[q, sem], ctx_recv.at[q, block], device_id={"ctx": to}, device_id_type=MESH
        )

    def finish(k):
        for at in range(0, columns, 128):
            span = slice(at, at + 128)
            stack[k, span, :] = (acc_all[k, :, span] / l_all[k, :1, span]).T.astype(jnp.bfloat16)
        for g in range(group):
            head = k * group + g
            out[:, head * hd : (head + 1) * hd] = stack[k, g * rows : (g + 1) * rows, :]

    def forward(q):
        if q % 2 == 0:

            @pl.when(c == 2)
            def _():
                along(q, 1, 0, 2).wait_recv()
                along(q, 1, 1, 3).start()

        else:

            @pl.when(c == 0)
            def _():
                along(q, 1, 1, 0).wait_recv()
                along(q, 1, 2, 3).start()

        @pl.when(c == 3)
        def _():
            along(q, 0, 0, 3).wait_recv()
            along(q, 0, 0, 2).start()

    def fold_earlier(p):
        def earlier(t, _):
            last = c // 3
            block = last * ((3 - t) % 3) + (1 - last) * (c - 1 - t)

            @pl.when((c == 1) | (t > 0))
            def _():
                along(2 * p, block, 0, c).wait_recv()

            @pl.when((c < 3) | (t > 0))
            def _():
                along(2 * p + 1, block, 0, c).wait_recv()

            attend(p, block, False)
            return 0

        lax.fori_loop(0, c, earlier, 0)
        if (p + 1) % HALVES == 0:
            finish(p // HALVES)

    for q in range(pieces):
        others = recvbuf[q].at[pl.ds(0, foreign)]
        pltpu.make_async_copy(others, others, page_recv.at[q]).wait()
        k, _, lanes = piece_of(q)
        own_part = q // 2 * ctx_count + c

        def place(j, _, q=q, lanes=lanes, own_part=own_part):
            at = idx[0, c * pages + j]
            spot = pl.ds(pl.multiple_of(j * run, run), run)
            page = recvbuf[q][at] * keep[q // 2 % HALVES, spot, :] + part[q // 2, spot, lanes]
            if q % 2 == 0:
                kv[own_part, spot, :] = page
            else:
                v_rows[spot, :] = page
            return 0

        lax.fori_loop(0, pages, place, 0)
        if q % 2 == 1:
            for i in range(0, length, 128):
                block = v_rows[i : i + 128, :].astype(jnp.float32)
                kv[own_part, length + i : length + i + 128, :] = block.T.astype(jnp.bfloat16)

        @pl.when(c == 0)
        def _(q=q):
            along(q, 0, 1, 3).start()
            along(q, 0, 0, 1).start()

        @pl.when(c == 1)
        def _(q=q):
            if q % 2 == 1:
                along(q, 1, 1, 0).start()
            along(q, 1, 0, 2).start()

        @pl.when(c == 2)
        def _(q=q):
            along(q, 2, 0, 3).start()

        send(q + AHEAD)

        if 0 < q < pieces - 1:
            forward(q - 1)
        if q % 2 == 1:
            attend(q // 2, c, True)
        elif q > 0:
            fold_earlier(q // 2 - 1)
        if q == pieces - 2:
            forward(q)
    forward(pieces - 1)
    fold_earlier(parts - 1)

    pltpu.make_async_copy(req.at[pl.ds(0, n - 1)], req.at[pl.ds(0, n - 1)], req_send).wait()
    for q in range(pieces):
        given = recvbuf[q].at[pl.ds(0, foreign)]
        pltpu.make_async_copy(given, given, page_send.at[q]).wait()
        if shared:
            passed = hop_in[q].at[pl.ds(0, PLANE - 1)]
            pltpu.make_async_copy(passed, passed, hop_send.at[q]).wait()

        @pl.when(c == 0)
        def _(q=q):
            along(q, 0, 0, 1).wait_send()
            along(q, 0, 1, 3).wait_send()
            if q % 2 == 1:
                along(q, 1, 2, 3).wait_send()

        @pl.when(c == 1)
        def _(q=q):
            along(q, 1, 0, 2).wait_send()
            if q % 2 == 1:
                along(q, 1, 1, 0).wait_send()

        @pl.when(c == 2)
        def _(q=q):
            along(q, 2, 0, 3).wait_send()
            if q % 2 == 0:
                along(q, 1, 1, 3).wait_send()

        @pl.when(c == 3)
        def _(q=q):
            along(q, 0, 0, 2).wait_send()


def shards(queries, fresh_kv, kv_store, page_owner, page_slot, rec_index):
    n, ctx_count = lax.axis_size("cache"), lax.axis_size("ctx")
    rows, kv_heads, hd = queries.shape[1], fresh_kv.shape[2], fresh_kv.shape[3] // 2
    heads = queries.shape[2] // hd
    slots, page_len = kv_store.shape[:2]
    pages_all = page_owner.shape[1]
    pages = pages_all // ctx_count
    parts, run = kv_heads * HALVES, page_len // HALVES
    pieces, length = 2 * parts, pages * run
    columns = heads // kv_heads * rows
    dims = (n, ctx_count, kv_heads, slots, pages, page_len, rows, heads, hd)
    bf16, f32, i32 = jnp.bfloat16, jnp.float32, jnp.int32
    vmem, hbm = pl.BlockSpec(memory_space=pltpu.VMEM), pl.BlockSpec(memory_space=pltpu.HBM)
    dma = pltpu.SemaphoreType.DMA
    def call(shared, *arrays):
        return pl.pallas_call(
            functools.partial(kernel, dims, shared),
            out_shape=[jax.ShapeDtypeStruct((rows, heads * hd), bf16), jax.ShapeDtypeStruct((1, 1), i32)],
            in_specs=[hbm] * 6,
            out_specs=[vmem, vmem],
            scratch_shapes=[
                pltpu.VMEM((1, pages_all), i32),
                pltpu.VMEM((1, pages_all), i32),
                pltpu.VMEM(rec_index.shape, i32),
                pltpu.VMEM((n, 1, 128), i32),
                pltpu.VMEM((n, 1, 128), i32),
                pltpu.SMEM((n, 1, 128), i32),
                pltpu.VMEM((8, pages_all), i32),
                pltpu.SMEM((8, pages_all), i32),
                pltpu.VMEM((slots, page_len, kv_heads, 2 * hd), bf16),
                pltpu.VMEM((rows, kv_heads, 2 * hd), bf16),
                pltpu.VMEM((rows, heads * hd), bf16),
                pltpu.VMEM((slots * kv_heads, page_len, 2 * hd), bf16),
                pltpu.VMEM((pieces, n, 2, run, hd), bf16),
                pltpu.VMEM((parts * ctx_count, 2 * length, hd), bf16),
                pltpu.VMEM((length, hd), bf16),
                pltpu.VMEM((1, columns), i32),
                pltpu.VMEM((kv_heads, rows, 2 * hd), bf16),
                pltpu.VMEM((parts, length, 2 * hd), bf16),
                pltpu.VMEM((HALVES, length, hd), bf16),
                pltpu.VMEM((kv_heads, columns, hd), bf16),
                pltpu.VMEM((kv_heads, hd, columns), bf16),
                pltpu.VMEM((kv_heads, 8, columns), f32),
                pltpu.VMEM((kv_heads, 8, columns), f32),
                pltpu.VMEM((kv_heads, hd, columns), f32),
                dma((6,)), dma, dma, dma((2,)),
                dma((pieces,)), dma((pieces,)),
                dma((pieces, 3)), dma((pieces, ctx_count)),
                dma((pieces,)), dma((pieces,)),
                pltpu.VMEM((pieces, PLANE, n // PLANE, run, hd), bf16),
                pltpu.VMEM((pieces, n // PLANE, SPARE, run, hd), bf16),
                *[pltpu.VMEM((2 * n, run, hd), bf16) for _ in range(pieces)],
                *[pltpu.VMEM((PLANE, n // PLANE, run, hd), bf16) for _ in range(pieces)],
            ],
            compiler_params=pltpu.CompilerParams(
                collective_id=0 if shared else 1, has_side_effects=True, vmem_limit_bytes=60 * 1024 * 1024
            ),
        )(*arrays)

    arrays = (page_owner[:, :, 0], page_slot, rec_index, kv_store, fresh_kv[0], queries[0])
    result, over = call(True, *arrays)
    result = lax.cond(over[0, 0] > 0, lambda: call(False, *arrays)[0], lambda: result)
    return result[None]


def solution(mesh):
    in_specs = (
        P("cache", "ctx", "head"),
        P("cache", "ctx", "head", None),
        P("cache", None, "head", None),
        P("cache", None, None),
        P("cache", None),
        P("cache", None),
    )
    out_specs = P("cache", "ctx", "head")
    return jax.shard_map(shards, mesh=mesh, in_specs=in_specs, out_specs=out_specs, check_vma=False)
```

```python
import functools
import math

import jax
import jax.numpy as jnp
from jax import lax
from jax.experimental import pallas as pl
from jax.experimental.pallas import tpu as pltpu
from jax.sharding import PartitionSpec as P

MESH = pl.DeviceIdType.MESH
EMPTY = -1e30
HIDDEN = -2e30
HALVES = 2
AHEAD = 3
LEAD = 2
PLANE = 4
SPARE = 2


def kernel(
    dims, shared, owner_in, slot_in, rec_hbm, raw_in, fresh_in, queries_in, out, over,
    owner_row, slot_row, rec_in, req, req_in, req_smem, idx_rows, idx, raw, fresh_raw, queries, store, sendbuf, kv, v_rows, rec_tiled,
    fresh, part, keep, stack, q_t, m_all, l_all, acc_all,
    load_sem, req_send, req_recv, smem_sem, page_send, page_recv, ctx_send, ctx_recv, hop_send, hop_recv,
    hop_out, spare_out, *landing,
):
    n, ctx_count, kv_heads, slots, pages, page_len, rows, heads, hd = dims
    parts = kv_heads * HALVES
    pieces = parts * 2
    run = page_len // HALVES
    length = pages * run
    group = heads // kv_heads
    columns = group * rows
    pages_all = pages * ctx_count
    recvbuf, hop_in = landing[:pieces], landing[pieces:]
    planes = n // PLANE
    i32 = jnp.int32
    me = lax.axis_index("cache")
    c = lax.axis_index("ctx")

    arrays = (
        (owner_in, owner_row), (slot_in, slot_row), (raw_in, raw),
        (rec_hbm, rec_in), (fresh_in, fresh_raw), (queries_in, queries),
    )
    loads = [pltpu.make_async_copy(src, dst, load_sem.at[i]) for i, (src, dst) in enumerate(arrays)]
    for load in loads:
        load.start()

    barrier = pltpu.get_barrier_semaphore()

    def greet(k, _):
        pl.semaphore_signal(barrier, inc=1, device_id={"cache": lax.rem(me + k, n)}, device_id_type=MESH)
        return 0

    lax.fori_loop(1, n, greet, 0)
    for step in (1, ctx_count - 1):
        pl.semaphore_signal(barrier, inc=1, device_id={"ctx": lax.rem(c + step, ctx_count)}, device_id_type=MESH)

    a = lax.broadcasted_iota(i32, (pages_all, pages_all), 0)
    b = lax.broadcasted_iota(i32, (pages_all, pages_all), 1)
    loads[0].wait()
    loads[1].wait()
    owner = owner_row[...]
    owner_f = jnp.broadcast_to(owner, (pages_all, pages_all)).astype(jnp.float32)
    owner_of_a = jnp.sum(jnp.where(a == b, owner_f, 0.0), axis=1, keepdims=True).astype(i32)
    low = c * pages
    one_block = a // pages == b // pages
    alike = (owner_of_a == owner) & one_block
    second = jnp.max(jnp.where(alike & (a < b), 1, 0), axis=0, keepdims=True)
    if shared:
        second_of_a = jnp.max(jnp.where(alike & (b < a), 1.0, 0.0), axis=1, keepdims=True)
        beside = one_block & (owner_of_a // PLANE == owner // PLANE) & (second_of_a > 0.5)
        lowest = jnp.min(jnp.where(beside, owner_of_a % PLANE, PLANE), axis=0, keepdims=True)
        spare = n + owner // PLANE * SPARE + jnp.where(owner % PLANE == lowest, 0, 1)
        where_to = jnp.where(second > 0, spare, owner)
    else:
        where_to = owner * 2 + second
    idx_rows[...] = jnp.broadcast_to(where_to, idx_rows.shape)
    to_idx = pltpu.make_async_copy(idx_rows, idx, smem_sem.at[0])
    to_idx.start()

    shard = lax.broadcasted_iota(i32, (n, pages_all), 0)
    place_of = lax.broadcasted_iota(i32, (n, pages_all), 1)
    named = (shard == owner) & (place_of >= low) & (place_of < low + pages)
    coded = (place_of * slots + slot_row[...]).astype(jnp.float32)
    first = jnp.min(jnp.where(named, coded, float(pages_all * slots)), axis=1, keepdims=True)
    final = jnp.max(jnp.where(named, coded, 0.0), axis=1, keepdims=True)
    asked = jnp.where(place_of == 0, first, final).astype(i32) % slots
    if shared:
        mine = (shard // PLANE == owner // PLANE) & (second > 0)
        here = mine & (place_of >= low) & (place_of < low + pages)
        member = (owner % PLANE).astype(jnp.float32)
        least = jnp.min(jnp.where(here, member, float(PLANE)), axis=1, keepdims=True).astype(i32) % PLANE
        most = jnp.max(jnp.where(here, member, 0.0), axis=1, keepdims=True).astype(i32) % PLANE
        excess = jnp.zeros((n, 1), jnp.float32)
        for other in range(ctx_count):
            there = mine & (place_of // pages == other)
            excess = jnp.maximum(excess, jnp.sum(jnp.where(there, 1.0, 0.0), axis=1, keepdims=True))
        excess = jnp.max(excess, axis=0, keepdims=True)
        asked = jnp.where(place_of == 2, least, asked)
        asked = jnp.where(place_of == 3, most, asked)
        asked = jnp.where(place_of >= 4, jnp.where(excess > SPARE, 1, 0), asked)
    for d in range(n):
        req[d] = asked[d : d + 1, :]

    loads[2].wait()

    def split(p, _):
        store[pl.ds(p * kv_heads, kv_heads)] = jnp.swapaxes(raw[p], 0, 1)
        return 0

    lax.fori_loop(0, slots, split, 0)
    to_idx.wait()
    pl.semaphore_wait(barrier, n + 1)

    def ask(k, _):
        d = lax.rem(me + k, n)
        pltpu.make_async_remote_copy(
            req.at[d], req_in.at[me], req_send, req_recv, device_id={"cache": d}, device_id_type=MESH
        ).start()
        return 0

    lax.fori_loop(1, n, ask, 0)
    req_in[me] = req[me]

    loads[3].wait()
    fresh_pos = jnp.zeros((1, rows), i32)
    for other in range(ctx_count):
        theirs = rec_in[:, other * rows : (other + 1) * rows]
        fresh_pos = jnp.where(c == other, theirs, fresh_pos)
    for g in range(group):
        rec_tiled[:, g * rows : (g + 1) * rows] = fresh_pos
    loads[4].wait()
    by_head = jnp.swapaxes(fresh_raw[...], 0, 1)
    for k in range(kv_heads):
        fresh[k] = by_head[k]
    for half in range(HALVES):
        local = lax.broadcasted_iota(jnp.int32, (length, rows), 0)
        pos = (local // run) * page_len + half * run + local % run
        hit = jnp.where(pos == fresh_pos, 1.0, 0.0)
        covered = jnp.sum(hit, axis=1, keepdims=True)
        keep[half] = jnp.broadcast_to(1.0 - covered, (length, hd)).astype(jnp.bfloat16)
        one_hot = hit.astype(jnp.bfloat16)
        for k in range(kv_heads):
            part[k * HALVES + half] = jnp.dot(
                one_hot, fresh[k], preferred_element_type=jnp.float32
            ).astype(jnp.bfloat16)

    others = req_in.at[pl.ds(0, n - 1)]
    pltpu.make_async_copy(others, others, req_recv).wait()
    to_smem = pltpu.make_async_copy(req_in, req_smem, smem_sem.at[1])
    to_smem.start()
    flags = jnp.max(req_in[...], axis=0).astype(jnp.float32)
    over[...] = jnp.max(flags[:, 4:], axis=1, keepdims=True).astype(i32)
    to_smem.wait()

    def piece_of(q):
        half, which = q // 2 % HALVES, q % 2
        return q // (2 * HALVES), slice(half * run, (half + 1) * run), slice(which * hd, (which + 1) * hd)

    def page(q, d, r):
        k, span, lanes = piece_of(q)
        return store[req_smem[d, 0, r] * kv_heads + k, span, lanes]

    z, m = me // PLANE, me % PLANE

    def mate_copy(q, mate):
        return pltpu.make_async_remote_copy(
            hop_out.at[q, mate], hop_in[q].at[m], hop_send.at[q], hop_recv.at[q],
            device_id={"cache": z * PLANE + mate}, device_id_type=MESH,
        )

    def to_mates(q):
        def fill(i, _):
            for mate in range(PLANE):
                hop_out[q, mate, i] = page(q, i * PLANE + mate, 1)
            hop_in[q][m, i] = page(q, i * PLANE + m, 1)
            return 0

        lax.fori_loop(0, planes, fill, 0)
        for t in range(1, PLANE):
            mate_copy(q, (m + t) % PLANE).start()

    def give_first(q):
        def give(step, _):
            d = lax.rem(me + step, n)
            sendbuf[q, d, 0] = page(q, d, 0)
            pltpu.make_async_remote_copy(
                sendbuf.at[q, d, 0], recvbuf[q].at[me], page_send.at[q], page_recv.at[q],
                device_id={"cache": d}, device_id_type=MESH,
            ).start()
            return 0

        lax.fori_loop(1, n, give, 0)
        recvbuf[q][me] = page(q, me, 0)

    def give_spare(q):
        arrived = hop_in[q].at[pl.ds(0, PLANE - 1)]
        pltpu.make_async_copy(arrived, arrived, hop_recv.at[q]).wait()

        def give(step, _):
            i = lax.rem(z + step, planes)
            d = i * PLANE + m
            for e in range(SPARE):
                spare_out[q, i, e] = hop_in[q][req_smem[d, 0, 2 + e] & (PLANE - 1), i]
            pltpu.make_async_remote_copy(
                spare_out.at[q, i], recvbuf[q].at[pl.ds(n + z * SPARE, SPARE)], page_send.at[q], page_recv.at[q],
                device_id={"cache": d}, device_id_type=MESH,
            ).start()
            return 0

        lax.fori_loop(1, planes, give, 0)
        for e in range(SPARE):
            recvbuf[q][n + z * SPARE + e] = hop_in[q][req_smem[me, 0, 2 + e] & (PLANE - 1), z]

    def give_both(q):
        def give(step, _):
            d = lax.rem(me + step, n)
            for r in range(2):
                sendbuf[q, d, r] = page(q, d, r)
            pltpu.make_async_remote_copy(
                sendbuf.at[q, d], recvbuf[q].at[pl.ds(me * 2, 2)], page_send.at[q], page_recv.at[q],
                device_id={"cache": d}, device_id_type=MESH,
            ).start()
            return 0

        lax.fori_loop(1, n, give, 0)
        for r in range(2):
            recvbuf[q][me * 2 + r] = page(q, me, r)

    def send(q):
        if shared:
            if q < pieces:
                give_first(q)
            if q + LEAD < pieces:
                to_mates(q + LEAD)
            if 0 < q <= pieces:
                give_spare(q - 1)
        elif q < pieces:
            give_both(q)

    if shared:
        for q in range(LEAD):
            to_mates(q)
    for q in range(AHEAD):
        send(q)
    foreign = n - 1 + (planes - 1) * SPARE if shared else 2 * (n - 1)

    loads[5].wait()
    for g in range(heads):
        at = (g % group) * rows
        stack[g // group, at : at + rows, :] = queries[:, g * hd : (g + 1) * hd]
    for k in range(kv_heads):
        for at in range(0, columns, 128):
            block = stack[k, at : at + 128, :].astype(jnp.float32)
            q_t[k, :, at : at + 128] = block.T.astype(jnp.bfloat16)
    m_all[...] = jnp.full(m_all.shape, EMPTY, jnp.float32)
    l_all[...] = jnp.zeros(l_all.shape, jnp.float32)
    acc_all[...] = jnp.zeros(acc_all.shape, jnp.float32)

    factor = hd**-0.5 * math.log2(math.e)

    def attend(q, block, own):
        k = q // HALVES
        at = q * ctx_count + block
        keys = kv[at, :length, :]
        values = jnp.concatenate(
            [kv[at, length + i : length + i + 128, :] for i in range(0, length, 128)], axis=1
        )
        scores = jnp.dot(keys, q_t[k], preferred_element_type=jnp.float32)
        if own:
            local = lax.broadcasted_iota(jnp.int32, (length, 1), 0)
            pos = (local // run) * page_len + (q % HALVES) * run + local % run
            scores = jnp.where(pos <= rec_tiled[...], scores, HIDDEN)
        m_old = m_all[k]
        m_new = jnp.maximum(m_old, jnp.max(scores, axis=0, keepdims=True))
        alpha = jnp.exp2((m_old - m_new) * factor)
        weights = jnp.exp2((scores - m_new[:1]) * factor)
        l_all[k] = l_all[k] * alpha + jnp.sum(weights, axis=0, keepdims=True)
        acc_all[k] = acc_all[k] * alpha[:1] + jnp.dot(
            values, weights.astype(jnp.bfloat16), preferred_element_type=jnp.float32
        )
        m_all[k] = m_new

    def along(q, block, sem, to):
        ref = kv.at[q // 2 * ctx_count + block, pl.ds(q % 2 * length, length)]
        return pltpu.make_async_remote_copy(
            ref, ref, ctx_send.at[q, sem], ctx_recv.at[q, block], device_id={"ctx": to}, device_id_type=MESH
        )

    def finish(k):
        for at in range(0, columns, 128):
            span = slice(at, at + 128)
            stack[k, span, :] = (acc_all[k, :, span] / l_all[k, :1, span]).T.astype(jnp.bfloat16)
        for g in range(group):
            head = k * group + g
            out[:, head * hd : (head + 1) * hd] = stack[k, g * rows : (g + 1) * rows, :]

    def forward(q):
        if q % 2 == 0:

            @pl.when(c == 2)
            def _():
                along(q, 1, 0, 2).wait_recv()
                along(q, 1, 1, 3).start()

        else:

            @pl.when(c == 0)
            def _():
                along(q, 1, 1, 0).wait_recv()
                along(q, 1, 2, 3).start()

        @pl.when(c == 3)
        def _():
            along(q, 0, 0, 3).wait_recv()
            along(q, 0, 0, 2).start()

    def fold_earlier(p):
        def earlier(t, _):
            last = c // 3
            block = last * ((3 - t) % 3) + (1 - last) * (c - 1 - t)

            @pl.when((c == 1) | (t > 0))
            def _():
                along(2 * p, block, 0, c).wait_recv()

            @pl.when((c < 3) | (t > 0))
            def _():
                along(2 * p + 1, block, 0, c).wait_recv()

            attend(p, block, False)
            return 0

        lax.fori_loop(0, c, earlier, 0)
        if (p + 1) % HALVES == 0:
            finish(p // HALVES)

    for q in range(pieces):
        others = recvbuf[q].at[pl.ds(0, foreign)]
        pltpu.make_async_copy(others, others, page_recv.at[q]).wait()
        k, _, lanes = piece_of(q)
        own_part = q // 2 * ctx_count + c

        def place(j, _, q=q, lanes=lanes, own_part=own_part):
            at = idx[0, c * pages + j]
            spot = pl.ds(pl.multiple_of(j * run, run), run)
            page = recvbuf[q][at] * keep[q // 2 % HALVES, spot, :] + part[q // 2, spot, lanes]
            if q % 2 == 0:
                kv[own_part, spot, :] = page
            else:
                v_rows[spot, :] = page
            return 0

        lax.fori_loop(0, pages, place, 0)
        if q % 2 == 1:
            for i in range(0, length, 128):
                block = v_rows[i : i + 128, :].astype(jnp.float32)
                kv[own_part, length + i : length + i + 128, :] = block.T.astype(jnp.bfloat16)

        @pl.when(c == 0)
        def _(q=q):
            along(q, 0, 1, 3).start()
            along(q, 0, 0, 1).start()

        @pl.when(c == 1)
        def _(q=q):
            if q % 2 == 1:
                along(q, 1, 1, 0).start()
            along(q, 1, 0, 2).start()

        @pl.when(c == 2)
        def _(q=q):
            along(q, 2, 0, 3).start()

        send(q + AHEAD)

        if 0 < q < pieces - 1:
            forward(q - 1)
        if q % 2 == 1:
            attend(q // 2, c, True)
        elif q > 0:
            fold_earlier(q // 2 - 1)
        if q == pieces - 2:
            forward(q)
    forward(pieces - 1)
    fold_earlier(parts - 1)

    pltpu.make_async_copy(req.at[pl.ds(0, n - 1)], req.at[pl.ds(0, n - 1)], req_send).wait()
    for q in range(pieces):
        given = recvbuf[q].at[pl.ds(0, foreign)]
        pltpu.make_async_copy(given, given, page_send.at[q]).wait()
        if shared:
            passed = hop_in[q].at[pl.ds(0, PLANE - 1)]
            pltpu.make_async_copy(passed, passed, hop_send.at[q]).wait()

        @pl.when(c == 0)
        def _(q=q):
            along(q, 0, 0, 1).wait_send()
            along(q, 0, 1, 3).wait_send()
            if q % 2 == 1:
                along(q, 1, 2, 3).wait_send()

        @pl.when(c == 1)
        def _(q=q):
            along(q, 1, 0, 2).wait_send()
            if q % 2 == 1:
                along(q, 1, 1, 0).wait_send()

        @pl.when(c == 2)
        def _(q=q):
            along(q, 2, 0, 3).wait_send()
            if q % 2 == 0:
                along(q, 1, 1, 3).wait_send()

        @pl.when(c == 3)
        def _(q=q):
            along(q, 0, 0, 2).wait_send()


def shards(queries, fresh_kv, kv_store, page_owner, page_slot, rec_index):
    n, ctx_count = lax.axis_size("cache"), lax.axis_size("ctx")
    rows, kv_heads, hd = queries.shape[1], fresh_kv.shape[2], fresh_kv.shape[3] // 2
    heads = queries.shape[2] // hd
    slots, page_len = kv_store.shape[:2]
    pages_all = page_owner.shape[1]
    pages = pages_all // ctx_count
    parts, run = kv_heads * HALVES, page_len // HALVES
    pieces, length = 2 * parts, pages * run
    columns = heads // kv_heads * rows
    dims = (n, ctx_count, kv_heads, slots, pages, page_len, rows, heads, hd)
    bf16, f32, i32 = jnp.bfloat16, jnp.float32, jnp.int32
    vmem, hbm = pl.BlockSpec(memory_space=pltpu.VMEM), pl.BlockSpec(memory_space=pltpu.HBM)
    dma = pltpu.SemaphoreType.DMA
    def call(shared, *arrays):
        return pl.pallas_call(
            functools.partial(kernel, dims, shared),
            out_shape=[jax.ShapeDtypeStruct((rows, heads * hd), bf16), jax.ShapeDtypeStruct((1, 1), i32)],
            in_specs=[hbm] * 6,
            out_specs=[vmem, vmem],
            scratch_shapes=[
                pltpu.VMEM((1, pages_all), i32),
                pltpu.VMEM((1, pages_all), i32),
                pltpu.VMEM(rec_index.shape, i32),
                pltpu.VMEM((n, 1, 128), i32),
                pltpu.VMEM((n, 1, 128), i32),
                pltpu.SMEM((n, 1, 128), i32),
                pltpu.VMEM((8, pages_all), i32),
                pltpu.SMEM((8, pages_all), i32),
                pltpu.VMEM((slots, page_len, kv_heads, 2 * hd), bf16),
                pltpu.VMEM((rows, kv_heads, 2 * hd), bf16),
                pltpu.VMEM((rows, heads * hd), bf16),
                pltpu.VMEM((slots * kv_heads, page_len, 2 * hd), bf16),
                pltpu.VMEM((pieces, n, 2, run, hd), bf16),
                pltpu.VMEM((parts * ctx_count, 2 * length, hd), bf16),
                pltpu.VMEM((length, hd), bf16),
                pltpu.VMEM((1, columns), i32),
                pltpu.VMEM((kv_heads, rows, 2 * hd), bf16),
                pltpu.VMEM((parts, length, 2 * hd), bf16),
                pltpu.VMEM((HALVES, length, hd), bf16),
                pltpu.VMEM((kv_heads, columns, hd), bf16),
                pltpu.VMEM((kv_heads, hd, columns), bf16),
                pltpu.VMEM((kv_heads, 8, columns), f32),
                pltpu.VMEM((kv_heads, 8, columns), f32),
                pltpu.VMEM((kv_heads, hd, columns), f32),
                dma((6,)), dma, dma, dma((2,)),
                dma((pieces,)), dma((pieces,)),
                dma((pieces, 3)), dma((pieces, ctx_count)),
                dma((pieces,)), dma((pieces,)),
                pltpu.VMEM((pieces, PLANE, n // PLANE, run, hd), bf16),
                pltpu.VMEM((pieces, n // PLANE, SPARE, run, hd), bf16),
                *[pltpu.VMEM((2 * n, run, hd), bf16) for _ in range(pieces)],
                *[pltpu.VMEM((PLANE, n // PLANE, run, hd), bf16) for _ in range(pieces)],
            ],
            compiler_params=pltpu.CompilerParams(
                collective_id=0 if shared else 1, has_side_effects=True, vmem_limit_bytes=60 * 1024 * 1024
            ),
        )(*arrays)

    arrays = (page_owner[:, :, 0], page_slot, rec_index, kv_store, fresh_kv[0], queries[0])
    result, over = call(True, *arrays)
    result = lax.cond(over[0, 0] > 0, lambda: call(False, *arrays)[0], lambda: result)
    return result[None]


def solution(mesh):
    in_specs = (
        P("cache", "ctx", "head"),
        P("cache", "ctx", "head", None),
        P("cache", None, "head", None),
        P("cache", None, None),
        P("cache", None),
        P("cache", None),
    )
    out_specs = P("cache", "ctx", "head")
    return jax.shard_map(shards, mesh=mesh, in_specs=in_specs, out_specs=out_specs, check_vma=False)
```
